128 devices in a mesh: dp: 8 (over x, core), expert: 16 (over z, y).
Axes of the slice: x: 4, y: 4, z: 4, core: 2. Of those that a mesh axis runs over, the one named last changes fastest.
Arguments:
- tokens: bfloat16 [32768, 7168], P(('dp', 'expert')), may hold values from -6 to 6
- routes: int32 [32768, 2], P(('dp', 'expert')), may hold values from 0 to 15, all different within a row; in each aligned block of 256 rows (0 to 255, 256 to 511, ...) at most 64 rows name the same one
- weight: bfloat16 [16, 2048, 7168], P('expert', 'dp'), may hold values from -6 to 6
- levels: int32 [16, 2048], P('expert', 'dp'), may hold values from 4 to 16
- pivots: float32 [16, 128], P('expert'), may hold values from 0.5 to 1.5
- panel_diag: float32 [16, 128, 128], P('expert'), may hold values from -1.5 to 1.5
- panel_rest: float32 [16, 128, 7040], P('expert', None, 'dp'), may hold values from -1.5 to 1.5
Outputs:
- hessian: float32 [16, 512, 7168], P('expert', 'dp')
- quantized: float32 [16, 2048, 128], P('expert', 'dp')
- remainder: float32 [16, 2048, 7040], P('expert', 'dp')
The draws below stay inside these ranges and needn't reach their ends.
Inputs may be any that keep to these rules, and one draw needn't show every extreme that they name: `routes`: the 2 experts of a token differ. Among the rows of one device no expert is named by more than 64 tokens, and some device's rows name some expert exactly 64 times. Every expert is named by some token.
All inputs are finite; a program needn't handle non-finite values.
Results may differ from the reference program's by a relative error of at most 0.00055.
Values may be sent and summed in bfloat16 or wider, within the bound.
No kernel may reach another device: no remote copies, remote signals or barrier semaphores. Data moves between devices by JAX's collectives and lax.ppermute only.
A program may use at most 128 MiB of HBM per device.

```python
import math
import jax
import jax.numpy as jnp
import numpy as np
from jax import lax

D = 7168
FF = 2048
TOK_DEV = 256
TOPK = 2
HROWS = 512
BLOCK = 128
EXPERTS = 16
CAP = 64
TOKENS = 32768
N_DP = 8
N_EXPERT = 16


def set_ends(values, key, smallest, top_value):
    extent = values.shape
    spot = [jax.random.randint(jax.random.fold_in(key, axis), (), 0, extent[axis]) for axis in range(len(extent))]
    values = values.at[tuple(spot)].set(smallest)
    longest = extent.index(max(extent))
    spot[longest] = (spot[longest] + 1) % extent[longest]
    return values.at[tuple(spot)].set(top_value)


def block_levels(own_key, shape, split, smallest, top_value):
    loudness, own = 1.0, jax.random.fold_in(own_key, 6)
    for dim, parts in split:
        steps = jnp.exp(jax.random.uniform(jax.random.fold_in(own, dim), (parts,), jnp.float32, smallest / len(split), top_value / len(split)))
        loudness = loudness * jnp.repeat(steps, shape[dim] // parts).reshape([-1 if axis == dim else 1 for axis in range(len(shape))])
    return loudness


def deal_out(key, own, number, rows, amount, top, most, slope):
    order = jax.random.permutation(key, amount)
    packed, usual = load_shares(amount, rows * top, most, slope, True), load_shares(amount, rows * top, most, slope, False)
    places = jnp.arange(amount)

    def named(tallies, rotation):
        used = int((tallies > 0).sum())
        fixed = max(1, used // 4)
        shifted = fixed + (places - fixed + rotation * (used - fixed)) % max(1, amount - fixed)
        return jnp.zeros((amount,), jnp.int32).at[order[jnp.where(places < fixed, places, shifted)]].set(jnp.asarray(tallies, jnp.int32))

    tallies = jnp.where(number % 4 == 0, named(packed, number // 4), named(usual, number - number // 4 - 1))
    mixed = jax.random.permutation(jax.random.fold_in(own, 3), amount)
    donor, taker = mixed[0:amount // 2 * 2:2], mixed[1:amount // 2 * 2:2]
    margin = jnp.minimum(tallies[donor] - 1, most - tallies[taker]) // 2
    margin = jnp.where((donor == order[0]) | (taker == order[0]) | (tallies[taker] == 0), 0, jnp.maximum(margin, 0))
    shifted = jax.random.randint(jax.random.fold_in(own, 4), (amount // 2,), 0, 1 << 20) % (margin + 1)
    tallies = tallies.at[donor].add(-shifted).at[taker].add(shifted)
    labels = jnp.searchsorted(jnp.cumsum(tallies), jnp.arange(rows * top), side="right").astype(jnp.int32)
    grid = labels.reshape(top, rows).T
    grid = grid[jax.random.permutation(jax.random.fold_in(own, 1), rows)]
    rotation = jax.random.randint(jax.random.fold_in(own, 2), (rows, 1), 0, top)
    return jnp.take_along_axis(grid, (jnp.arange(top)[None, :] + rotation) % top, axis=1)


def load_shares(amount, total, most, lean, full):
    weights = [(1 << 20) // math.isqrt(rank ** lean) + 1 for rank in range(1, amount + 1)]
    largest = most if full else min(most, max(-(-total // amount), total * weights[0] // sum(weights)))
    least = 1 if total - largest >= amount - 1 else 0
    given, spare = [largest] + [least] * (amount - 1), total - largest - least * (amount - 1)
    while spare > 0:
        movable = [i for i in range(1, amount) if given[i] < largest] or [i for i in range(1, amount) if given[i] < most]
        whole, budget = sum([weights[i] for i in movable]), spare
        for i in movable:
            addition = min(most - given[i], max(1, budget * weights[i] // whole), spare)
            given[i] = given[i] + addition
            spare = spare - addition
    return np.array(given)


def scatter_about(own_key, shape, scale, bound, pieces=(), held_as=jnp.bfloat16):
    gain = block_levels(own_key, shape, pieces, -0.22, 0.18) if pieces else 1.0
    array = jax.random.normal(own_key, shape, jnp.float32) * scale * gain
    return jnp.minimum(jnp.maximum(array, -bound), bound).astype(held_as)


def setup_inputs(seed: int = 0) -> dict:
    arg_keys = jax.random.split(jax.random.key(seed), 8)
    tokens = scatter_about(arg_keys[0], (TOKENS, D), 1.0, 6.0, ((0, 128),))
    routes_keys = jax.random.split(jax.random.fold_in(arg_keys[1], 1), TOKENS // TOK_DEV)
    routes_turns = jax.random.permutation(jax.random.fold_in(arg_keys[1], 3), TOKENS // TOK_DEV)
    routes = jax.vmap(lambda own, number: deal_out(jax.random.fold_in(arg_keys[1], 2), own, number, TOK_DEV, EXPERTS, TOPK, CAP, 2))(routes_keys, routes_turns).reshape((TOKENS, TOPK))
    weight = scatter_about(arg_keys[2], (EXPERTS, FF, D), 1.0, 6.0, ((0, 16), (1, 8)))
    levels = set_ends(jax.random.randint(arg_keys[3], (EXPERTS, FF), 4, 17), jax.random.fold_in(arg_keys[3], 1), 4, 16).astype(jnp.int32)
    pivots = jnp.clip(jnp.exp(math.log(1.5) - 1.0986123 * jax.random.uniform(arg_keys[4], (EXPERTS, BLOCK), jnp.float32) ** block_levels(arg_keys[4], (EXPERTS, BLOCK), ((0, 16),), -0.2, 0.2)), 0.5, 1.5)
    panel_diag = scatter_about(arg_keys[5], (EXPERTS, BLOCK, BLOCK), 0.1, 1.5, ((0, 16),), jnp.float32)
    panel_rest = scatter_about(arg_keys[6], (EXPERTS, BLOCK, D - BLOCK), 0.1, 1.5, ((0, 16), (2, 8)), jnp.float32)
    return {"tokens": tokens, "routes": routes, "weight": weight, "levels": levels, "pivots": pivots, "panel_diag": panel_diag, "panel_rest": panel_rest}


def smooth_grid(values, spacing):
    return values - 0.9 * spacing / (2.0 * math.pi) * jnp.sin(2.0 * math.pi * values / spacing)


def block_update(block_cols, spacing, strict_upper, pivots):
    width = block_cols.shape[1]

    def advance(column, carry):
        current, snapped_all, errors = carry
        column = jnp.asarray(column).astype(jnp.int32)
        values = lax.dynamic_slice_in_dim(current, column, 1, 1)
        snapped = smooth_grid(values, spacing)
        scaled = (values - snapped) / lax.dynamic_slice_in_dim(pivots, column, 1, 0)[None, :]
        upper_row = lax.dynamic_slice_in_dim(strict_upper, column, 1, 0)
        current = current - scaled * upper_row
        snapped_all = lax.dynamic_update_slice_in_dim(snapped_all, snapped, column, 1)
        errors = lax.dynamic_update_slice_in_dim(errors, scaled, column, 1)
        return current, snapped_all, errors

    zeros = jnp.zeros_like(block_cols)
    final_block, snapped_all, errors = lax.fori_loop(0, width, advance, (block_cols, zeros, zeros))
    return snapped_all, errors


def quantize_rows(weight_rows, level_rows, pivots, panel_diag, panel_rest):
    block_cols = weight_rows[:, :BLOCK].astype(jnp.float32)
    spacing = (jnp.max(jnp.abs(block_cols), axis=1, keepdims=True) + 1e-5) / level_rows.astype(jnp.float32)[:, None]
    strict_upper = jnp.triu(panel_diag, 1)
    snapped_all, errors = block_update(block_cols, spacing, strict_upper, pivots)
    later = weight_rows[:, BLOCK:].astype(jnp.float32)
    remainder = later - jnp.dot(errors, panel_rest, precision=lax.Precision.HIGHEST, preferred_element_type=jnp.float32)
    return snapped_all, remainder


def reference(tokens, routes, weight, levels, pivots, panel_diag, panel_rest):
    most_rows = N_DP * N_EXPERT * CAP

    def gram_one(expert_id):
        member = jnp.any(routes == expert_id, axis=1)
        member_count = jnp.sum(member.astype(jnp.int32))
        picked = jnp.nonzero(member, size=most_rows, fill_value=0)[0].astype(jnp.int32)
        keep = (jnp.arange(most_rows, dtype=jnp.int32) < member_count).astype(jnp.float32)
        chosen = tokens[picked].astype(jnp.float32) * keep[:, None]
        slab = jnp.dot(chosen[:, :HROWS].T, chosen, precision=lax.Precision.HIGHEST, preferred_element_type=jnp.float32)
        return slab * (2.0 / member_count.astype(jnp.float32))

    hessian = lax.map(gram_one, jnp.arange(EXPERTS, dtype=jnp.int32))

    def quantize_one(items):
        return quantize_rows(items[0], items[1], items[2], items[3], items[4])

    quantized, remainder = lax.map(quantize_one, (weight, levels, pivots, panel_diag, panel_rest))
    return hessian, quantized, remainder
```

```python
import functools
import math

import jax
import jax.numpy as jnp
import numpy as np
from jax import lax
from jax.experimental import pallas as pl
from jax.experimental.pallas import tpu as pltpu
from jax.sharding import Mesh
from jax.sharding import PartitionSpec as P

BLOCK = 128
PLANE = ("z", "y")
EXPERTS = 16
TOK = 256
CAP = 64
MIB = 1024 * 1024
UP = [(i, (i + 1) % 4) for i in range(4)]
DOWN = [(i, (i - 1) % 4) for i in range(4)]
OPPOSITE = [(i, (i + 2) % 4) for i in range(4)]
SWAP = [(0, 1), (1, 0)]
bf16, f16, f32, i32 = jnp.bfloat16, jnp.float16, jnp.float32, jnp.int32
SLAB_ROWS, ROUTE_ROWS = 4 * TOK, 16
FIRST_ROWS = SLAB_ROWS + ROUTE_ROWS + 2 * TOK
SECOND_ROWS = TOK + TOK // 2
EXTRA = 16


def sine_coefficients():
    nodes = 0.5 * np.cos(np.pi * (np.arange(400) + 0.5) / 800)
    powers = np.stack([nodes ** (2 * k + 1) for k in range(8)], 1)
    scale = 1.0 / np.abs(powers).max(0)
    fit = np.linalg.lstsq(powers * scale, np.sin(2 * np.pi * nodes), rcond=None)[0]
    return [float(c) for c in fit * scale]


SINE = sine_coefficients()


def sine_turns(turns):
    r = turns - jnp.round(turns)
    s = r * r
    total = jnp.full_like(r, SINE[-1])
    for c in SINE[-2::-1]:
        total = total * s + c
    return total * r


def build_kernel(slab_ref, a_ref, b_ref, c_ref, d_ref, routes_ref, first_ref, second_ref):
    first_ref[0, :512, :] = slab_ref[:, :128]
    first_ref[0, 512:SLAB_ROWS, :] = slab_ref[:, 128:]
    first_ref[0, SLAB_ROWS : SLAB_ROWS + ROUTE_ROWS, :] = routes_ref[...]
    start = SLAB_ROWS + ROUTE_ROWS
    first_ref[0, start : start + TOK, :] = a_ref[...]
    first_ref[0, start + TOK : start + 2 * TOK, :] = b_ref[...]
    second_ref[0, :TOK, :] = c_ref[...]
    last = d_ref[...].astype(f32)
    turned = pltpu.roll(last, 64, 1)
    even = lax.rem(pl.program_id(0), 2) == 0
    low = lax.broadcasted_iota(i32, (128, 128), 1) < 64
    left, right = jnp.where(even, last, turned), jnp.where(even, turned, last)
    second_ref[0, TOK:, :] = jnp.where(low, left[:128], right[128:]).astype(bf16)


def build(tokens, routes_rows):
    return pl.pallas_call(
        build_kernel,
        grid=(EXPERTS,),
        in_specs=[
            pl.BlockSpec((512, TOK), lambda i: (0, 0)),
            pl.BlockSpec((TOK, 128), lambda i: (0, i)),
            pl.BlockSpec((TOK, 128), lambda i: (0, EXPERTS + i)),
            pl.BlockSpec((TOK, 128), lambda i: (0, 2 * EXPERTS + i)),
            pl.BlockSpec((TOK, 128), lambda i: (0, 3 * EXPERTS + i // 2)),
            pl.BlockSpec((ROUTE_ROWS, 128), lambda i: (0, 0)),
        ],
        out_specs=[
            pl.BlockSpec((1, FIRST_ROWS, 128), lambda i: (i, 0, 0)),
            pl.BlockSpec((1, SECOND_ROWS, 128), lambda i: (i, 0, 0)),
        ],
        out_shape=[
            pltpu.HBM((EXPERTS, FIRST_ROWS, 128), bf16),
            pltpu.HBM((EXPERTS, SECOND_ROWS, 128), bf16),
        ],
        compiler_params=pltpu.CompilerParams(vmem_limit_bytes=48 * MIB),
        name="build",
    )(tokens[:, :512].T, *[pltpu.with_memory_space_constraint(tokens, pltpu.HBM)] * 4, routes_rows)


def places_of(routes_rows):
    rows = routes_rows.astype(f32)
    one = jnp.concatenate([rows[0:1], rows[1:2]], axis=1)
    two = jnp.concatenate([rows[2:3], rows[3:4]], axis=1)
    expert = lax.broadcasted_iota(i32, (EXPERTS, TOK), 0).astype(f32)
    member = jnp.where((one == expert) | (two == expert), 1.0, 0.0)
    before = lax.broadcasted_iota(i32, (TOK, TOK), 0) < lax.broadcasted_iota(i32, (TOK, TOK), 1)
    earlier = jnp.dot(
        member.astype(bf16), jnp.where(before, 1.0, 0.0).astype(bf16), preferred_element_type=f32
    )
    return jnp.where(member > 0, earlier, -1.0)


def fill_pick(places, pick_ref, flip):
    slot = lax.broadcasted_iota(i32, (CAP, TOK), 0).astype(f32)
    for e in range(EXPERTS):
        hit = jnp.broadcast_to(places[e : e + 1, :], (CAP, TOK)) == slot
        to = (e ^ flip) * CAP
        pick_ref[to : to + CAP, :] = jnp.where(hit, 1.0, 0.0).astype(bf16)


def split_rows(here_ref, part_ref, keep_ref, send_ref, store):
    x, core = here_ref[0], here_ref[1]
    for step in range(4):
        owner = lax.rem(x + step, 4) * 2
        store(keep_ref, step, part_ref[owner + core])
        store(send_ref, step, part_ref[owner + 1 - core])


def note_largest(top_ref, product):
    largest = jnp.max(jnp.abs(product).reshape(-1, 8, product.shape[1]), axis=0)
    top_ref[...] = jnp.maximum(top_ref[...], jnp.maximum(largest[:, :128], largest[:, 128:]))


def slots_of_pair(pair, blocks, cols, picks, slab, held):
    for source in range(2):
        places = places_of(blocks[source][SLAB_ROWS : SLAB_ROWS + ROUTE_ROWS, :])
        fill_pick(places, picks[source], source)
    low = lax.broadcasted_iota(i32, (512, 128), 1) < CAP
    lanes = pl.ds(pl.multiple_of(pair * 128, 128), 128)
    rows = [jnp.concatenate([block[:512, :], block[512:SLAB_ROWS, :]], axis=1) for block in blocks]
    for quarter in range(4):
        got = [
            lax.dot_general(
                rows[source],
                picks[source][quarter * 256 : (quarter + 1) * 256, :],
                (((1,), (1,)), ((), ())),
                preferred_element_type=f32,
            ).astype(bf16)
            for source in range(2)
        ]
        for half in range(2):
            m = 2 * quarter + half
            a, b = (g[:, half * 128 : (half + 1) * 128] for g in got)
            slab[2 * m, :, lanes] = jnp.where(low, a, b)
            slab[2 * m + 1, :, lanes] = jnp.where(low, b, a)
    for quarter in range(4):
        got = [
            jnp.dot(
                picks[source][quarter * 256 : (quarter + 1) * 256, :],
                cols[source],
                preferred_element_type=f32,
            ).astype(bf16)
            for source in range(2)
        ]
        for source in range(2):
            for block in range(4):
                e = (4 * quarter + block) ^ source
                offset = CAP * ((e + source) % 2)
                held[e, pl.ds(pl.multiple_of(pair * 128 + offset, CAP), CAP), :] = got[source][
                    block * CAP : (block + 1) * CAP
                ]


def product0_kernel(here_ref, in_ref, keep_ref, send_ref, top_ref, pick0, pick1, slab, held, part):
    step = pl.program_id(0)

    @pl.when(step == 0)
    def _():
        top_ref[...] = jnp.zeros_like(top_ref)

    @pl.when(step < 8)
    def _():
        blocks = [in_ref.at[source] for source in range(2)]
        start = SLAB_ROWS + ROUTE_ROWS
        cols = [
            jnp.concatenate(
                [block[start : start + TOK, :], block[start + TOK : start + 2 * TOK, :]], axis=1
            )
            for block in blocks
        ]
        slots_of_pair(step, blocks, cols, (pick0, pick1), slab, held)

    @pl.when(step >= 8)
    def _():
        products = [
            jnp.dot(slab[e], held[e], preferred_element_type=f32)
            for e in (2 * (step - 8), 2 * (step - 8) + 1)
        ]
        for k in range(2):
            note_largest(top_ref, products[k])
            part[k] = products[k].reshape(8, 64, 256)
        for k in range(2):

            def store(ref, at, value):
                ref[at, k * 64 : (k + 1) * 64] = value

            split_rows(here_ref, part.at[k], keep_ref, send_ref, store)


SCRATCH = [
    pltpu.VMEM((1024, TOK), bf16),
    pltpu.VMEM((1024, TOK), bf16),
    pltpu.VMEM((EXPERTS, 512, 1024), bf16),
    pltpu.VMEM((EXPERTS, 1024, 256), bf16),
    pltpu.VMEM((2, 8, 64, 256), f32),
]


def early(i, here):
    return (jnp.minimum(i, 7), 0, 0)


def product0(here, first):
    rows = pl.BlockSpec((4, 128, 256), lambda i, here: (0, jnp.maximum(i - 8, 0), 0))
    return pl.pallas_call(
        product0_kernel,
        grid_spec=pltpu.PrefetchScalarGridSpec(
            num_scalar_prefetch=1,
            grid=(16,),
            in_specs=[pl.BlockSpec((2, FIRST_ROWS, 128), early)],
            out_specs=[rows, rows, pl.BlockSpec((8, 128), lambda i, here: (0, 0))],
            scratch_shapes=SCRATCH,
        ),
        out_shape=[pltpu.HBM((4, EXPERTS * 64 + EXTRA, 256), f32)] * 2
        + [jax.ShapeDtypeStruct((8, 128), f32)],
        compiler_params=pltpu.CompilerParams(vmem_limit_bytes=40 * MIB),
        cost_estimate=pl.CostEstimate(flops=11 * 10**9, bytes_accessed=16 * 10**6, transcendentals=0),
        name="product0",
    )(here, first)


def product1_kernel(
    here_ref, in_ref, cols_ref, keep_ref, send_ref, top_ref, pick0, pick1, slab, held, part
):
    step = pl.program_id(0)

    @pl.when(step == 0)
    def _():
        top_ref[...] = jnp.zeros_like(top_ref)

    @pl.when(step < 8)
    def _():
        blocks = [in_ref.at[source] for source in range(2)]
        cols = []
        for source in range(2):
            last = cols_ref[source, TOK:, :]
            turned = pltpu.roll(last.astype(f32), 64, 1).astype(bf16)
            last = jnp.concatenate([last, turned], axis=0)
            cols.append(jnp.concatenate([cols_ref[source, :TOK, :], last], axis=1))
        slots_of_pair(step, blocks, cols, (pick0, pick1), slab, held)

    @pl.when(step >= 8)
    def _():
        experts = (2 * (step - 8), 2 * (step - 8) + 1)
        products = [jnp.dot(slab[e], held[e], preferred_element_type=f32) for e in experts]
        for k in range(2):
            note_largest(top_ref, products[k])
            part[k] = products[k].reshape(8, 64, 256)
        for k in range(2):

            def store(ref, at, value):
                ref[at, pl.ds(pl.multiple_of(experts[k] * 64, 64), 64)] = value[:, :128]

            split_rows(here_ref, part.at[k], keep_ref, send_ref, store)

        low = lax.broadcasted_iota(i32, (512, 128), 1) < 64
        both = jnp.where(low, products[0][:, 128:], pltpu.roll(products[1][:, 128:], 64, 1))
        part[0, :, :, :128] = both.reshape(8, 64, 128)

        def store_last(ref, at, value):
            start = EXPERTS * 64 + (step - 8) * 64
            ref[at, pl.ds(pl.multiple_of(start, 64), 64)] = value[:, :128]

        split_rows(here_ref, part.at[0], keep_ref, send_ref, store_last)


def product1(here, first, second):
    rows = pl.BlockSpec(
        (4, 24 * 64 + EXTRA, 128), lambda i, here: (0, 0, 0), pipeline_mode=pl.Buffered(1)
    )
    return pl.pallas_call(
        product1_kernel,
        grid_spec=pltpu.PrefetchScalarGridSpec(
            num_scalar_prefetch=1,
            grid=(16,),
            in_specs=[
                pl.BlockSpec((2, FIRST_ROWS, 128), early),
                pl.BlockSpec((2, SECOND_ROWS, 128), early),
            ],
            out_specs=[rows, rows, pl.BlockSpec((8, 128), lambda i, here: (0, 0))],
            scratch_shapes=SCRATCH,
        ),
        out_shape=[pltpu.HBM((4, 24 * 64 + EXTRA, 128), f32)] * 2
        + [jax.ShapeDtypeStruct((8, 128), f32)],
        compiler_params=pltpu.CompilerParams(vmem_limit_bytes=44 * MIB),
        cost_estimate=pl.CostEstimate(flops=11 * 10**9, bytes_accessed=16 * 10**6, transcendentals=0),
        name="product1",
    )(here, first, second)


def sum_over_core(keep, send, top):
    other = lax.ppermute(send, "core", SWAP)
    top = jnp.max(top) + jnp.max(lax.ppermute(top, "core", SWAP))
    exponent = jnp.clip(jnp.floor(jnp.log2(32000.0 / jnp.maximum(top, 1e-30))), -100.0, 100.0)
    factor = jnp.exp2(exponent)
    rows = keep.shape[1] - EXTRA
    value = lax.broadcasted_iota(i32, keep.shape[1:], 0) < rows
    others = [
        jnp.where(value, (keep[i] + other[i]) * factor, exponent).astype(f16) for i in (1, 2, 3)
    ]
    return (keep[0], other[0]), others


def sum_over_x(own, others):
    rows = own[0].shape[0] - EXTRA

    def wide(value):
        return value.astype(f32) * jnp.exp2(-value[rows : rows + 1].astype(f32))

    one, two, three = others
    return ((own[0] + own[1] + wide(two)) + (wide(one) + wide(three)))[:rows]


def over_x(others):
    return [lax.ppermute(value, "x", pairs) for value, pairs in zip(others, (UP, OPPOSITE, DOWN))]


def over_dp(value):
    a, b, c = (lax.ppermute(value, "x", pairs) for pairs in (UP, OPPOSITE, DOWN))
    value = (value + b) + (a + c)
    return value + lax.ppermute(value, "core", SWAP)


def order_kernel(half_ref, scale_ref, a_ref, b_ref, out_ref):
    scale = scale_ref[0]
    half = half_ref[0]
    for i in range(EXPERTS):
        out_ref[:, i * 128 : (i + 1) * 128] = a_ref[i, :, :128] * scale
        out_ref[:, (16 + i) * 128 : (17 + i) * 128] = a_ref[i, :, 128:] * scale
        out_ref[:, (32 + i) * 128 : (33 + i) * 128] = b_ref[i, :64, :] * scale
    low = lax.broadcasted_iota(i32, (64, 128), 1) < 64
    for t in range(8):
        left, right = b_ref[2 * t, 64:, :], b_ref[2 * t + 1, 64:, :]
        even = jnp.where(low, left, pltpu.roll(right, 64, 1))
        odd = jnp.where(low, pltpu.roll(left, 64, 1), right)
        out_ref[:, (48 + t) * 128 : (49 + t) * 128] = jnp.where(half == 0, even, odd) * scale


def put_in_order(half, scale, a, b):
    smem, vmem = pl.BlockSpec(memory_space=pltpu.SMEM), pl.BlockSpec(memory_space=pltpu.VMEM)
    return pl.pallas_call(
        order_kernel,
        in_specs=[smem, smem, vmem, vmem],
        out_specs=vmem,
        out_shape=jax.ShapeDtypeStruct((64, 7168), f32),
        compiler_params=pltpu.CompilerParams(vmem_limit_bytes=16 * MIB),
        name="put_in_order",
    )(half, scale, a, b)


def columns_kernel(block_ref, levels_ref, pivots_ref, upper_ref, turned_ref, snapped_ref, errors_ref, now, out, err):
    block = block_ref[...].astype(f32).T
    now[...] = block
    largest = jnp.max(jnp.abs(block), axis=0, keepdims=True)
    spacing = (largest + 1e-05) / levels_ref[...].astype(f32)
    per_turn = 1.0 / spacing
    reach = 0.9 * spacing / (2.0 * math.pi)
    lane = lax.broadcasted_iota(i32, (8, BLOCK), 1)

    def group(b, carry):
        at = pl.multiple_of(b * 8, 8)
        tile = now[pl.ds(at, 8), :]
        turned = turned_ref[pl.ds(at, 8), :]
        near = [
            jnp.sum(jnp.where(lane == at + i, turned, 0.0), axis=1, keepdims=True) for i in range(8)
        ]
        snapped, errors = [], []
        for i in range(8):
            values = tile[i : i + 1, :]
            moved = values - reach * sine_turns(values * per_turn)
            error = (values - moved) * pivots_ref[at + i]
            tile = tile - near[i] * error
            snapped.append(moved)
            errors.append(error)
        errors = jnp.concatenate(errors, axis=0)
        out[pl.ds(at, 8), :] = jnp.concatenate(snapped, axis=0)
        err[pl.ds(at, 8), :] = errors
        now[...] -= lax.dot_general(
            upper_ref[pl.ds(at, 8), :],
            errors,
            (((0,), (0,)), ((), ())),
            precision=lax.Precision.HIGHEST,
            preferred_element_type=f32,
        )
        return carry

    lax.fori_loop(0, BLOCK // 8, group, 0)
    snapped_ref[...] = out[...].T
    errors_ref[...] = err[...].T


def block_update(rows, levels, pivots, upper):
    whole = lambda *shape: pl.BlockSpec(shape, lambda i: (0,) * len(shape))
    count = rows.shape[0]
    return pl.pallas_call(
        columns_kernel,
        grid=(1,),
        in_specs=[
            whole(count, BLOCK),
            whole(1, count),
            pl.BlockSpec(memory_space=pltpu.SMEM),
            whole(BLOCK, BLOCK),
            whole(BLOCK, BLOCK),
        ],
        out_specs=[whole(count, BLOCK)] * 2,
        out_shape=[jax.ShapeDtypeStruct((count, BLOCK), f32)] * 2,
        scratch_shapes=[pltpu.VMEM((BLOCK, count), f32)] * 3,
        compiler_params=pltpu.CompilerParams(vmem_limit_bytes=16 * MIB),
        cost_estimate=pl.CostEstimate(flops=10**9, bytes_accessed=2 * 10**6, transcendentals=0),
        name="block_update",
    )(rows, levels, 1.0 / pivots, upper, upper.T)


def panel_over_x(panel):
    mine = panel.T.astype(bf16)
    return [mine] + [lax.ppermute(mine, "x", pairs) for pairs in (DOWN, OPPOSITE, UP)]


def whole_panel(ahead, x, first):
    other = list(lax.ppermute(jnp.stack(ahead), "core", SWAP))
    pieces = []
    for at in range(4):
        mine, theirs = (lax.select_n(lax.rem(at + 4 - x, 4), *parts) for parts in (ahead, other))
        pieces += [jnp.where(first, mine, theirs), jnp.where(first, theirs, mine)]
    return jnp.concatenate(pieces, axis=0)


def later_kernel(errors_ref, panel_ref, *refs):
    *weight_refs, out_ref, done_ref = refs
    errors = errors_ref[...]
    panel = panel_ref[...]
    total = None
    for _ in range(3):
        part = errors.astype(bf16)
        errors = errors - part.astype(f32)
        product = lax.dot_general(part, panel, (((1,), (1,)), ((), ())), preferred_element_type=f32)
        total = product if total is None else total + product
    for k, ref in enumerate(weight_refs):
        out_ref[:, k * 128 : (k + 1) * 128] = ref[...].astype(f32) - total[:, k * 128 : (k + 1) * 128]
    done_ref[...] = jnp.zeros_like(done_ref)


def later_columns(rows, errors, panel):
    count, later = rows.shape[0], panel.shape[0]
    columns = [
        pl.BlockSpec((count, 128), functools.partial(lambda k, i: (0, 5 * i + k), k)) for k in range(1, 6)
    ]
    return pl.pallas_call(
        later_kernel,
        grid=(later // 640,),
        in_specs=[
            pl.BlockSpec((count, BLOCK), lambda i: (0, 0)),
            pl.BlockSpec((640, BLOCK), lambda i: (i, 0)),
        ]
        + columns,
        out_specs=[
            pl.BlockSpec((count, 640), lambda i: (0, i)),
            pl.BlockSpec((8, 128), lambda i: (0, 0)),
        ],
        out_shape=[pltpu.HBM((count, later), f32), jax.ShapeDtypeStruct((8, 128), f32)],
        compiler_params=pltpu.CompilerParams(vmem_limit_bytes=16 * MIB),
        cost_estimate=pl.CostEstimate(flops=15 * 10**8, bytes_accessed=13 * 10**6, transcendentals=0),
        name="later_columns",
    )(errors, panel, *[rows] * 5)


def on_device(tokens, routes, weight, levels, pivots, panel_diag, panel_rest):
    x, core = lax.axis_index("x"), lax.axis_index("core")
    place = lax.axis_index("z") * 4 + lax.axis_index("y")
    routes_rows = jnp.pad(routes.T.reshape(4, 128).astype(bf16), ((0, ROUTE_ROWS - 4), (0, 0)))
    exchange = functools.partial(
        lax.all_to_all, axis_name=PLANE, split_axis=0, concat_axis=0, tiled=True
    )
    here = jnp.stack([x, core]).astype(i32)
    half = lax.rem(place, 2).astype(i32)[None]
    first_core = core == 0

    first, second = build(tokens, routes_rows)
    first, here, half, place, x, first_core, pivots = lax.optimization_barrier(
        (first, here, half, place, x, first_core, pivots)
    )
    first = exchange(first)
    first, second, weight, levels, panel_diag, panel_rest, pivots = lax.optimization_barrier(
        (first, second, weight, levels, panel_diag, panel_rest, pivots)
    )
    second = exchange(second)
    keep, send, top = product0(here, first)
    send, top, second, weight, panel_rest = lax.optimization_barrier(
        (send, top, second, weight, panel_rest)
    )
    own, others = sum_over_core(keep, send, top)

    rows = weight[0]
    upper = jnp.triu(panel_diag[0], 1)
    snapped, errors = block_update(rows, levels, pivots[0], upper)
    panel = panel_over_x(panel_rest[0])

    first, second, others, panel, errors = lax.optimization_barrier(
        (first, second, others, panel, errors)
    )
    others = over_x(others)
    keep, send, top = product1(here, first, second)
    keep, send, top, others, rows, panel, first = lax.optimization_barrier(
        (keep, send, top, others, rows, panel, first)
    )
    total = exchange(sum_over_x(own, others).reshape(EXPERTS, 64, 256))
    own, others = sum_over_core(keep, send, top)

    others, rows, errors, panel, first = lax.optimization_barrier((others, rows, errors, panel, first))
    others = over_x(others)
    remainder, done = later_columns(rows, errors, whole_panel(panel, x, first_core))
    others, done = lax.optimization_barrier((others, done))

    named = first[:, SLAB_ROWS : SLAB_ROWS + 4, :].reshape(1, -1).astype(f32)
    counts = jnp.sum(
        (named == lax.broadcasted_iota(i32, (EXPERTS, 1), 0).astype(f32)).astype(f32), axis=1
    )
    counts = over_dp(jnp.broadcast_to(jnp.pad(counts, (0, 128 - EXPERTS)), (8, 128)))[0]
    own_count = lax.dynamic_index_in_dim(counts, place, 0, keepdims=True)

    tail = sum_over_x(own, others).reshape(24, 64, 128)
    tail = exchange(
        jnp.concatenate([tail[:EXPERTS], jnp.repeat(tail[EXPERTS:], 2, axis=0)], axis=1)
    )
    hessian = put_in_order(half, 2.0 / own_count, total, tail)
    return hessian[None], snapped[None], remainder[None]


def solution(mesh):
    devices = mesh.devices
    fine = Mesh(devices.reshape(4, 2, 4, 4), ("x", "core", "z", "y"))
    dp, every = ("x", "core"), ("x", "core", "z", "y")
    return jax.shard_map(
        on_device,
        mesh=fine,
        in_specs=(
            P(every, None),
            P(every, None),
            P(PLANE, dp, None),
            P(PLANE, dp),
            P(PLANE, None),
            P(PLANE, None, None),
            P(PLANE, None, dp),
        ),
        out_specs=(P(PLANE, dp, None),) * 3,
        check_vma=False,
    )
```

```python
import functools
import math

import jax
import jax.numpy as jnp
import numpy as np
from jax import lax
from jax.experimental import pallas as pl
from jax.experimental.pallas import tpu as pltpu
from jax.sharding import Mesh
from jax.sharding import PartitionSpec as P

BLOCK = 128
PLANE = ("z", "y")
EXPERTS = 16
TOK = 256
CAP = 64
MIB = 1024 * 1024
UP = [(i, (i + 1) % 4) for i in range(4)]
DOWN = [(i, (i - 1) % 4) for i in range(4)]
OPPOSITE = [(i, (i + 2) % 4) for i in range(4)]
SWAP = [(0, 1), (1, 0)]
bf16, f16, f32, i32 = jnp.bfloat16, jnp.float16, jnp.float32, jnp.int32
SLAB_ROWS, ROUTE_ROWS = 4 * TOK, 16
FIRST_ROWS = SLAB_ROWS + ROUTE_ROWS + 2 * TOK
SECOND_ROWS = TOK + TOK // 2
EXTRA = 16


def sine_coefficients():
    nodes = 0.5 * np.cos(np.pi * (np.arange(400) + 0.5) / 800)
    powers = np.stack([nodes ** (2 * k + 1) for k in range(8)], 1)
    scale = 1.0 / np.abs(powers).max(0)
    fit = np.linalg.lstsq(powers * scale, np.sin(2 * np.pi * nodes), rcond=None)[0]
    return [float(c) for c in fit * scale]


SINE = sine_coefficients()


def sine_turns(turns):
    r = turns - jnp.round(turns)
    s = r * r
    total = jnp.full_like(r, SINE[-1])
    for c in SINE[-2::-1]:
        total = total * s + c
    return total * r


def build_kernel(tokens_ref, routes_ref, first_ref, second_ref, slab):
    i = pl.program_id(0)

    @pl.when(i == 0)
    def _():
        for tile in range(4):
            turned = tokens_ref[:, tile * 128 : (tile + 1) * 128].astype(f32).T.astype(bf16)
            slab[tile * 128 : (tile + 1) * 128, :] = turned[:, :128]
            slab[512 + tile * 128 : 512 + (tile + 1) * 128, :] = turned[:, 128:]

    def tile(k):
        return tokens_ref[:, pl.ds(pl.multiple_of(k * 128, 128), 128)]

    low = lax.broadcasted_iota(i32, (128, 128), 1) < 64
    last = tile(3 * EXPERTS + i).astype(f32)
    turned = pltpu.roll(last, 64, 1)
    for half, (left, right) in enumerate(((last, turned), (turned, last))):
        to = 2 * i + half
        first_ref[half, :SLAB_ROWS, :] = slab[...]
        first_ref[half, SLAB_ROWS : SLAB_ROWS + ROUTE_ROWS, :] = routes_ref[...]
        start = SLAB_ROWS + ROUTE_ROWS
        first_ref[half, start : start + TOK, :] = tile(to)
        first_ref[half, start + TOK : start + 2 * TOK, :] = tile(EXPERTS + to)
        second_ref[half, :TOK, :] = tile(2 * EXPERTS + to)
        second_ref[half, TOK:, :] = jnp.where(low, left[:128], right[128:]).astype(bf16)


def build(tokens, routes_rows):
    return pl.pallas_call(
        build_kernel,
        grid=(EXPERTS // 2,),
        in_specs=[
            pl.BlockSpec((TOK, tokens.shape[1]), lambda i: (0, 0)),
            pl.BlockSpec((ROUTE_ROWS, 128), lambda i: (0, 0)),
        ],
        out_specs=[
            pl.BlockSpec((2, FIRST_ROWS, 128), lambda i: (i, 0, 0)),
            pl.BlockSpec((2, SECOND_ROWS, 128), lambda i: (i, 0, 0)),
        ],
        out_shape=[
            pltpu.HBM((EXPERTS, FIRST_ROWS, 128), bf16),
            pltpu.HBM((EXPERTS, SECOND_ROWS, 128), bf16),
        ],
        scratch_shapes=[pltpu.VMEM((SLAB_ROWS, 128), bf16)],
        compiler_params=pltpu.CompilerParams(vmem_limit_bytes=24 * MIB),
        name="build",
    )(pltpu.with_memory_space_constraint(tokens, pltpu.HBM), routes_rows)


def places_of(routes_rows):
    rows = routes_rows.astype(f32)
    one = jnp.concatenate([rows[0:1], rows[1:2]], axis=1)
    two = jnp.concatenate([rows[2:3], rows[3:4]], axis=1)
    expert = lax.broadcasted_iota(i32, (EXPERTS, TOK), 0).astype(f32)
    member = jnp.where((one == expert) | (two == expert), 1.0, 0.0)
    before = lax.broadcasted_iota(i32, (TOK, TOK), 0) < lax.broadcasted_iota(i32, (TOK, TOK), 1)
    earlier = jnp.dot(
        member.astype(bf16), jnp.where(before, 1.0, 0.0).astype(bf16), preferred_element_type=f32
    )
    return jnp.where(member > 0, earlier, -1.0)


def fill_pick(places, pick_ref, flip):
    slot = lax.broadcasted_iota(i32, (CAP, TOK), 0).astype(f32)
    for e in range(EXPERTS):
        hit = jnp.broadcast_to(places[e : e + 1, :], (CAP, TOK)) == slot
        to = (e ^ flip) * CAP
        pick_ref[to : to + CAP, :] = jnp.where(hit, 1.0, 0.0).astype(bf16)


def split_rows(here_ref, part_ref, keep_ref, send_ref, store):
    x, core = here_ref[0], here_ref[1]
    for step in range(4):
        owner = lax.rem(x + step, 4) * 2
        store(keep_ref, step, part_ref[owner + core])
        store(send_ref, step, part_ref[owner + 1 - core])


def note_largest(top_ref, product):
    largest = jnp.max(jnp.abs(product).reshape(-1, 8, product.shape[1]), axis=0)
    top_ref[...] = jnp.maximum(top_ref[...], jnp.maximum(largest[:, :128], largest[:, 128:]))


def slab_in_slots(pair, blocks, picks, slab):
    low = lax.broadcasted_iota(i32, (512, 128), 1) < CAP
    lanes = pl.ds(pl.multiple_of(pair * 128, 128), 128)
    rows = [jnp.concatenate([block[:512, :], block[512:SLAB_ROWS, :]], axis=1) for block in blocks]
    for quarter in range(4):
        got = [
            lax.dot_general(
                rows[source],
                picks[source][quarter * 256 : (quarter + 1) * 256, :],
                (((1,), (1,)), ((), ())),
                preferred_element_type=f32,
            ).astype(bf16)
            for source in range(2)
        ]
        for half in range(2):
            m = 2 * quarter + half
            a, b = (g[:, half * 128 : (half + 1) * 128] for g in got)
            slab[2 * m, :, lanes] = jnp.where(low, a, b)
            slab[2 * m + 1, :, lanes] = jnp.where(low, b, a)


def columns_in_slots(pair, cols, picks, held):
    for quarter in range(4):
        got = [
            jnp.dot(
                picks[source][quarter * 256 : (quarter + 1) * 256, :],
                cols[source],
                preferred_element_type=f32,
            ).astype(bf16)
            for source in range(2)
        ]
        for source in range(2):
            for block in range(4):
                e = (4 * quarter + block) ^ source
                offset = CAP * ((e + source) % 2)
                held[e, pl.ds(pl.multiple_of(pair * 128 + offset, CAP), CAP), :] = got[source][
                    block * CAP : (block + 1) * CAP
                ]


def slab_copy(slab, out_ref, sems, pair):
    lanes = pl.ds(pl.multiple_of(pair * 128, 128), 128)
    return pltpu.make_async_copy(slab.at[:, :, lanes], out_ref.at[pair], sems.at[pair])


def finish_notes(top_ref, counts):
    largest = jnp.broadcast_to(jnp.max(top_ref[...], keepdims=True), top_ref.shape)
    top_ref[...] = jnp.where(lax.broadcasted_iota(i32, top_ref.shape, 0) == 0, largest, counts)


def count_tokens(routes_rows):
    rows = routes_rows.astype(f32)
    expert = lax.broadcasted_iota(i32, (128, 128), 0).astype(f32)
    named = sum(jnp.where(rows[k : k + 1] == expert, 1.0, 0.0) for k in range(4))
    return lax.dot_general(
        jnp.ones((8, 128), bf16),
        named.astype(bf16),
        (((1,), (1,)), ((), ())),
        preferred_element_type=f32,
    )


def product0_kernel(
    here_ref, in_ref, keep_ref, send_ref, top_ref, slab_ref, places_ref, pick0, pick1, held, slab, sems, part, counts
):
    step = pl.program_id(0)

    @pl.when(step == 0)
    def _():
        top_ref[...] = jnp.zeros_like(top_ref)
        counts[...] = jnp.zeros_like(counts)

    @pl.when(step < 8)
    def _():
        blocks = [in_ref.at[source] for source in range(2)]
        start = SLAB_ROWS + ROUTE_ROWS
        cols = [
            jnp.concatenate(
                [block[start : start + TOK, :], block[start + TOK : start + 2 * TOK, :]], axis=1
            )
            for block in blocks
        ]
        picks = (pick0, pick1)
        for source in range(2):
            routes_rows = blocks[source][SLAB_ROWS : SLAB_ROWS + ROUTE_ROWS, :]
            counts[...] += count_tokens(routes_rows)
            places = places_of(routes_rows)
            places_ref[source] = places
            fill_pick(places, picks[source], source)
        slab_in_slots(step, blocks, picks, slab)
        slab_copy(slab, slab_ref, sems, step).start()
        columns_in_slots(step, cols, picks, held)

    @pl.when(step >= 8)
    def _():
        products = [
            jnp.dot(slab[e], held[e], preferred_element_type=f32)
            for e in (2 * (step - 8), 2 * (step - 8) + 1)
        ]
        for k in range(2):
            note_largest(top_ref, products[k])
            for tile in range(2):
                rows = slice(tile * 64, (tile + 1) * 64)
                part[k, :, rows, :] = products[k][:, tile * 128 : (tile + 1) * 128].reshape(8, 64, 128)
        for k in range(2):

            def store(ref, at, value):
                ref[at, k * 128 : (k + 1) * 128] = value

            split_rows(here_ref, part.at[k], keep_ref, send_ref, store)

    @pl.when(step == 15)
    def _():
        finish_notes(top_ref, counts[...])
        for pair in range(8):
            slab_copy(slab, slab_ref, sems, pair).wait()


PICKS = [pltpu.VMEM((1024, TOK), bf16)] * 2
HELD = pltpu.VMEM((EXPERTS, 1024, 256), bf16)


def early(i, here):
    return (jnp.minimum(i, 7), 0, 0)


def product0(here, first):
    rows = pl.BlockSpec((4, 256, 128), lambda i, here: (0, jnp.maximum(i - 8, 0), 0))
    return pl.pallas_call(
        product0_kernel,
        grid_spec=pltpu.PrefetchScalarGridSpec(
            num_scalar_prefetch=1,
            grid=(16,),
            in_specs=[pl.BlockSpec((2, FIRST_ROWS, 128), early)],
            out_specs=[
                rows,
                rows,
                pl.BlockSpec((8, 128), lambda i, here: (0, 0)),
                pl.BlockSpec(memory_space=pl.ANY),
                pl.BlockSpec((2, EXPERTS, TOK), early),
            ],
            scratch_shapes=[
                *PICKS,
                HELD,
                pltpu.VMEM((EXPERTS, 512, 1024), bf16),
                pltpu.SemaphoreType.DMA((8,)),
                pltpu.VMEM((2, 8, 128, 128), f32),
                pltpu.VMEM((8, 128), f32),
            ],
        ),
        out_shape=[pltpu.HBM((4, EXPERTS * 128 + EXTRA, 128), f32)] * 2
        + [
            jax.ShapeDtypeStruct((8, 128), f32),
            pltpu.HBM((8, EXPERTS, 512, 128), bf16),
            jax.ShapeDtypeStruct((EXPERTS, EXPERTS, TOK), f32),
        ],
        compiler_params=pltpu.CompilerParams(vmem_limit_bytes=40 * MIB),
        cost_estimate=pl.CostEstimate(flops=11 * 10**9, bytes_accessed=16 * 10**6, transcendentals=0),
        name="product0",
    )(here, pltpu.with_memory_space_constraint(first, pltpu.HBM))


def product1_kernel(
    here_ref, places_ref, cols_ref, slab_ref, keep_ref, send_ref, top_ref, pick0, pick1, held, part, slab, sems
):
    step = pl.program_id(0)

    def fetch(pair):
        return pltpu.make_async_copy(
            slab_ref.at[:, pl.ds(2 * pair, 2)], slab.at[pair], sems.at[pair]
        )

    @pl.when(step == 0)
    def _():
        top_ref[...] = jnp.zeros_like(top_ref)
        for pair in range(8):
            fetch(pair).start()

    @pl.when(step < 8)
    def _():
        picks = (pick0, pick1)
        cols = []
        for source in range(2):
            fill_pick(places_ref[source], picks[source], source)
            last = cols_ref[source, TOK:, :]
            turned = pltpu.roll(last.astype(f32), 64, 1).astype(bf16)
            last = jnp.concatenate([last, turned], axis=0)
            cols.append(jnp.concatenate([cols_ref[source, :TOK, :], last], axis=1))
        columns_in_slots(step, cols, picks, held)

    @pl.when(step >= 8)
    def _():
        fetch(step - 8).wait()
        products = [
            jnp.dot(
                jnp.concatenate([slab[step - 8, pair, k] for pair in range(8)], axis=1),
                held[2 * (step - 8) + k],
                preferred_element_type=f32,
            )
            for k in range(2)
        ]
        low = lax.broadcasted_iota(i32, (8, 32, 128), 2) < 64
        for k in range(2):
            note_largest(top_ref, products[k])
            part[k, :, :64, :] = products[k][:, :128].reshape(8, 64, 128)
            halves = products[k][:, 128:].reshape(8, 2, 32, 128)
            turned = pltpu.roll(products[k][:, 128:], 64, 1).reshape(8, 2, 32, 128)
            part[k, :, 64:, :] = jnp.where(low, halves[:, 0], turned[:, 1])
        for k in range(2):

            def store(ref, at, value):
                ref[at, k * 96 : (k + 1) * 96] = value

            split_rows(here_ref, part.at[k], keep_ref, send_ref, store)

    @pl.when(step == 15)
    def _():
        finish_notes(top_ref, 0.0)


def product1(here, places, second, slab):
    rows = pl.BlockSpec((4, 192, 128), lambda i, here: (0, jnp.maximum(i - 8, 0), 0))
    return pl.pallas_call(
        product1_kernel,
        grid_spec=pltpu.PrefetchScalarGridSpec(
            num_scalar_prefetch=1,
            grid=(16,),
            in_specs=[
                pl.BlockSpec((2, EXPERTS, TOK), early),
                pl.BlockSpec((2, SECOND_ROWS, 128), early),
                pl.BlockSpec(memory_space=pl.ANY),
            ],
            out_specs=[rows, rows, pl.BlockSpec((8, 128), lambda i, here: (0, 0))],
            scratch_shapes=[
                *PICKS,
                HELD,
                pltpu.VMEM((2, 8, 96, 128), f32),
                pltpu.VMEM((8, 8, 2, 512, 128), bf16),
                pltpu.SemaphoreType.DMA((8,)),
            ],
        ),
        out_shape=[pltpu.HBM((4, EXPERTS * 96 + EXTRA, 128), f32)] * 2
        + [jax.ShapeDtypeStruct((8, 128), f32)],
        compiler_params=pltpu.CompilerParams(vmem_limit_bytes=40 * MIB),
        cost_estimate=pl.CostEstimate(flops=11 * 10**9, bytes_accessed=16 * 10**6, transcendentals=0),
        name="product1",
    )(here, places, second, slab)


def over_core(send, top):
    return lax.ppermute(send, "core", SWAP), top + lax.ppermute(top, "core", SWAP)


def sum_over_core(keep, other, top):
    top, counts = top[:1], top[1:2]
    exponent = jnp.clip(jnp.floor(jnp.log2(32000.0 / jnp.maximum(top, 1e-30))), -100.0, 100.0)
    exponent, factor = lax.optimization_barrier((exponent, jnp.exp2(exponent)))
    rows = keep.shape[1] - EXTRA
    row = lax.broadcasted_iota(i32, keep.shape[1:], 0)
    more = jnp.where(row == rows + 1, counts, exponent)
    others = [
        jnp.where(row < rows, (keep[i] + other[i]) * factor, more).astype(f16) for i in (1, 2, 3)
    ]
    return (keep[0], other[0], exponent, counts), others


def sum_over_x(own, others):
    rows = own[0].shape[0] - EXTRA
    exponents = [value[rows : rows + 1].astype(f32) for value in others]
    one, two, three = (
        value.astype(f32) * jnp.exp2(-exponent) for value, exponent in zip(others, exponents)
    )
    least = functools.reduce(jnp.minimum, exponents, own[2]) - 2.0
    total = (own[0] + own[1] + two) + (one + three)
    counts = own[3] + sum(value[rows + 1 : rows + 2].astype(f32) for value in others)
    return (total * jnp.exp2(least))[:rows].astype(f16), least, counts


def over_x(others):
    return [lax.ppermute(value, "x", pairs) for value, pairs in zip(others, (UP, OPPOSITE, DOWN))]


def order_kernel(scale_ref, a_ref, b_ref, out_ref):
    scale = scale_ref[0]
    for i in range(EXPERTS):
        out_ref[:, i * 128 : (i + 1) * 128] = a_ref[i, :64, :] * scale
        out_ref[:, (16 + i) * 128 : (17 + i) * 128] = a_ref[i, 64:, :] * scale
        out_ref[:, (32 + i) * 128 : (33 + i) * 128] = b_ref[i, :64, :] * scale
    low = lax.broadcasted_iota(i32, (32, 128), 1) < 64
    for t in range(8):
        left, right = b_ref[2 * t, 64:, :], b_ref[2 * t + 1, 64:, :]
        columns = slice((48 + t) * 128, (49 + t) * 128)
        out_ref[:32, columns] = jnp.where(low, left, pltpu.roll(right, 64, 1)) * scale
        out_ref[32:, columns] = jnp.where(low, pltpu.roll(left, 64, 1), right) * scale


def put_in_order(scale, a, b):
    smem, vmem = pl.BlockSpec(memory_space=pltpu.SMEM), pl.BlockSpec(memory_space=pltpu.VMEM)
    return pl.pallas_call(
        order_kernel,
        in_specs=[smem, vmem, vmem],
        out_specs=vmem,
        out_shape=jax.ShapeDtypeStruct((64, 7168), f32),
        compiler_params=pltpu.CompilerParams(vmem_limit_bytes=16 * MIB),
        name="put_in_order",
    )(scale, a, b)


def columns_kernel(block_ref, levels_ref, pivots_ref, upper_ref, turned_ref, snapped_ref, errors_ref, now, out, err):
    block = block_ref[...].astype(f32).T
    now[...] = block
    largest = jnp.max(jnp.abs(block), axis=0, keepdims=True)
    spacing = (largest + 1e-05) / levels_ref[...].astype(f32)
    per_turn = 1.0 / spacing
    reach = 0.9 * spacing / (2.0 * math.pi)
    lane = lax.broadcasted_iota(i32, (8, BLOCK), 1)

    def group(b, carry):
        at = pl.multiple_of(b * 8, 8)
        tile = now[pl.ds(at, 8), :]
        turned = turned_ref[pl.ds(at, 8), :]
        near = [
            jnp.sum(jnp.where(lane == at + i, turned, 0.0), axis=1, keepdims=True) for i in range(8)
        ]
        snapped, errors = [], []
        for i in range(8):
            values = tile[i : i + 1, :]
            moved = values - reach * sine_turns(values * per_turn)
            error = (values - moved) * pivots_ref[at + i]
            tile = tile - near[i] * error
            snapped.append(moved)
            errors.append(error)
        errors = jnp.concatenate(errors, axis=0)
        out[pl.ds(at, 8), :] = jnp.concatenate(snapped, axis=0)
        err[pl.ds(at, 8), :] = errors
        now[...] -= lax.dot_general(
            upper_ref[pl.ds(at, 8), :],
            errors,
            (((0,), (0,)), ((), ())),
            precision=lax.Precision.HIGHEST,
            preferred_element_type=f32,
        )
        return carry

    lax.fori_loop(0, BLOCK // 8, group, 0)
    snapped_ref[...] = out[...].T
    errors_ref[...] = err[...].T


def block_update(rows, levels, pivots, upper):
    whole = lambda *shape: pl.BlockSpec(shape, lambda i: (0,) * len(shape))
    count = rows.shape[0]
    return pl.pallas_call(
        columns_kernel,
        grid=(1,),
        in_specs=[
            whole(count, BLOCK),
            whole(1, count),
            pl.BlockSpec(memory_space=pltpu.SMEM),
            whole(BLOCK, BLOCK),
            whole(BLOCK, BLOCK),
        ],
        out_specs=[whole(count, BLOCK)] * 2,
        out_shape=[jax.ShapeDtypeStruct((count, BLOCK), f32)] * 2,
        scratch_shapes=[pltpu.VMEM((BLOCK, count), f32)] * 3,
        compiler_params=pltpu.CompilerParams(vmem_limit_bytes=16 * MIB),
        cost_estimate=pl.CostEstimate(flops=10**9, bytes_accessed=2 * 10**6, transcendentals=0),
        name="block_update",
    )(pltpu.with_memory_space_constraint(rows, pltpu.HBM), levels, 1.0 / pivots, upper, upper.T)


def ahead_over_x(mine):
    return [mine] + [lax.ppermute(mine, "x", pairs) for pairs in (DOWN, OPPOSITE, UP)]


def later_kernel(here_ref, errors_ref, own_ref, other_ref, *refs):
    *weight_refs, out_ref, panel, parts = refs
    i = pl.program_id(0)
    wide = panel.shape[0] // 8
    count = errors_ref.shape[0]

    @pl.when(i == 0)
    def _():
        x, core = here_ref[0], here_ref[1]
        for at in range(4):
            ahead = lax.rem(at + 4 - x, 4)
            mine = pl.multiple_of((2 * at + core) * wide, 16)
            theirs = pl.multiple_of((2 * at + 1 - core) * wide, 16)
            panel[pl.ds(mine, wide), :] = own_ref[ahead, :wide, :]
            panel[pl.ds(theirs, wide), :] = other_ref[ahead, :wide, :]
        errors = errors_ref[...]
        for k in range(3):
            part = errors.astype(bf16)
            errors = errors - part.astype(f32)
            parts[k * count : (k + 1) * count, :] = part

    got = lax.dot_general(
        parts[...],
        panel[pl.ds(pl.multiple_of(i * 640, 128), 640), :],
        (((1,), (1,)), ((), ())),
        preferred_element_type=f32,
    )
    total = (got[:count] + got[count : 2 * count]) + got[2 * count :]
    for k, ref in enumerate(weight_refs):
        out_ref[:, k * 128 : (k + 1) * 128] = ref[...].astype(f32) - total[:, k * 128 : (k + 1) * 128]


def later_columns(here, rows, errors, own, other):
    count, later = rows.shape[0], rows.shape[1] - BLOCK
    columns = [
        pl.BlockSpec((count, 128), functools.partial(lambda k, i, here: (0, 5 * i + k), k))
        for k in range(1, 6)
    ]
    whole = lambda a: pl.BlockSpec(a.shape, lambda i, here: (0,) * a.ndim)
    return pl.pallas_call(
        later_kernel,
        grid_spec=pltpu.PrefetchScalarGridSpec(
            num_scalar_prefetch=1,
            grid=(later // 640,),
            in_specs=[whole(errors), whole(own), whole(other)] + columns,
            out_specs=pl.BlockSpec((count, 640), lambda i, here: (0, i)),
            scratch_shapes=[pltpu.VMEM((later, BLOCK), bf16), pltpu.VMEM((3 * count, BLOCK), bf16)],
        ),
        out_shape=pltpu.HBM((count, later), f32),
        compiler_params=pltpu.CompilerParams(vmem_limit_bytes=24 * MIB),
        cost_estimate=pl.CostEstimate(flops=15 * 10**8, bytes_accessed=13 * 10**6, transcendentals=0),
        name="later_columns",
    )(here, errors, own, other, *[pltpu.with_memory_space_constraint(rows, pltpu.HBM)] * 5)


def on_device(tokens, routes, weight, levels, pivots, panel_diag, panel_rest):
    x, core = lax.axis_index("x"), lax.axis_index("core")
    place = lax.axis_index("z") * 4 + lax.axis_index("y")
    routes_rows = jnp.pad(routes.T.reshape(4, 128).astype(bf16), ((0, ROUTE_ROWS - 4), (0, 0)))
    exchange = functools.partial(
        lax.all_to_all, axis_name=PLANE, split_axis=0, concat_axis=0, tiled=True
    )
    here = jnp.stack([x, core]).astype(i32)

    first, second = build(tokens, routes_rows)
    first, here, place, pivots = lax.optimization_barrier((first, here, place, pivots))
    first = exchange(first)
    first, second, weight, levels, panel_diag, panel_rest, pivots = lax.optimization_barrier(
        (first, second, weight, levels, panel_diag, panel_rest, pivots)
    )
    second = exchange(second)
    keep, send, top, slab, places = product0(here, first)
    keep, send, top, second, slab, places, panel_rest = lax.optimization_barrier(
        (keep, send, top, second, slab, places, panel_rest)
    )
    panel = ahead_over_x(panel_rest[0].T.astype(bf16))
    own, others = sum_over_core(keep, *over_core(send, top))
    places, second, slab, others = lax.optimization_barrier((places, second, slab, others))
    others = over_x(others)
    keep, send, top = product1(here, places, second, slab)
    keep, send, top, others, panel, weight = lax.optimization_barrier(
        (keep, send, top, others, panel, weight)
    )
    total, least, counts = sum_over_x(own, others)
    panel = jnp.stack(panel)
    own, others = sum_over_core(keep, *over_core(send, top))

    others, rows, panel_diag, panel = lax.optimization_barrier((others, weight[0], panel_diag, panel))
    others = over_x(others)
    upper = jnp.triu(panel_diag[0], 1)
    snapped, errors = block_update(rows, levels, pivots[0], upper)
    other_panel = lax.ppermute(panel, "core", SWAP)
    others, errors, other_panel, total, least = lax.optimization_barrier(
        (others, errors, other_panel, total, least)
    )
    tail, last, _ = sum_over_x(own, others)
    sent = [total.reshape(EXPERTS, 128, 128), tail.reshape(EXPERTS, 96, 128)]
    first_rows = lax.broadcasted_iota(i32, (EXPERTS, 16, 128), 1) < 8
    sent.append(jnp.where(first_rows, least, last).astype(f16))
    sums = exchange(jnp.concatenate(sent, axis=1))

    remainder = later_columns(here, rows, errors, panel, other_panel)

    own_count = lax.dynamic_index_in_dim(counts[0], place, 0, keepdims=True)
    total = sums[:, :128].astype(f32) * jnp.exp2(-sums[:, 224:225].astype(f32))
    tail = sums[:, 128:224].astype(f32) * jnp.exp2(-sums[:, 232:233].astype(f32))
    hessian = put_in_order(2.0 / own_count, total, tail)
    return hessian[None], snapped[None], remainder[None]


def solution(mesh):
    devices = mesh.devices
    fine = Mesh(devices.reshape(4, 2, 4, 4), ("x", "core", "z", "y"))
    dp, every = ("x", "core"), ("x", "core", "z", "y")
    return jax.shard_map(
        on_device,
        mesh=fine,
        in_specs=(
            P(every, None),
            P(every, None),
            P(PLANE, dp, None),
            P(PLANE, dp),
            P(PLANE, None),
            P(PLANE, None, None),
            P(PLANE, None, dp),
        ),
        out_specs=(P(PLANE, dp, None),) * 3,
        check_vma=False,
    )
```

```python
import functools
import math

import jax
import jax.numpy as jnp
import numpy as np
from jax import lax
from jax.experimental import pallas as pl
from jax.experimental.pallas import tpu as pltpu
from jax.sharding import Mesh
from jax.sharding import PartitionSpec as P

BLOCK = 128
PLANE = ("z", "y")
EXPERTS = 16
TOK = 256
CAP = 64
MIB = 1024 * 1024
UP = [(i, (i + 1) % 4) for i in range(4)]
DOWN = [(i, (i - 1) % 4) for i in range(4)]
OPPOSITE = [(i, (i + 2) % 4) for i in range(4)]
SWAP = [(0, 1), (1, 0)]
bf16, f16, f32, i32 = jnp.bfloat16, jnp.float16, jnp.float32, jnp.int32
SLAB_ROWS, ROUTE_ROWS = 4 * TOK, 16
FIRST_ROWS = SLAB_ROWS + ROUTE_ROWS + 2 * TOK
SECOND_ROWS = TOK + TOK // 2
EXTRA = 16


def sine_coefficients():
    nodes = 0.5 * np.cos(np.pi * (np.arange(400) + 0.5) / 800)
    powers = np.stack([nodes ** (2 * k + 1) for k in range(8)], 1)
    scale = 1.0 / np.abs(powers).max(0)
    fit = np.linalg.lstsq(powers * scale, np.sin(2 * np.pi * nodes), rcond=None)[0]
    return [float(c) for c in fit * scale]


SINE = sine_coefficients()


def sine_turns(turns):
    r = turns - jnp.round(turns)
    s = r * r
    total = jnp.full_like(r, SINE[-1])
    for c in SINE[-2::-1]:
        total = total * s + c
    return total * r


def build_kernel(tokens_ref, routes_ref, first_ref, second_ref, slab):
    i = pl.program_id(0)
    routes = routes_ref[...].astype(f32)
    halves = [routes[k : k + 1, at : at + 128] for k in range(2) for at in (0, 128)]
    routes_rows = jnp.concatenate([*halves, jnp.zeros((ROUTE_ROWS - 4, 128), f32)], axis=0).astype(bf16)

    @pl.when(i == 0)
    def _():
        for tile in range(4):
            turned = tokens_ref[:, tile * 128 : (tile + 1) * 128].astype(f32).T.astype(bf16)
            slab[tile * 128 : (tile + 1) * 128, :] = turned[:, :128]
            slab[512 + tile * 128 : 512 + (tile + 1) * 128, :] = turned[:, 128:]

    def tile(k):
        return tokens_ref[:, pl.ds(pl.multiple_of(k * 128, 128), 128)]

    low = lax.broadcasted_iota(i32, (128, 128), 1) < 64
    last = tile(3 * EXPERTS + i).astype(f32)
    turned = pltpu.roll(last, 64, 1)
    for half, (left, right) in enumerate(((last, turned), (turned, last))):
        to = 2 * i + half
        first_ref[half, :SLAB_ROWS, :] = slab[...]
        first_ref[half, SLAB_ROWS : SLAB_ROWS + ROUTE_ROWS, :] = routes_rows
        start = SLAB_ROWS + ROUTE_ROWS
        first_ref[half, start : start + TOK, :] = tile(to)
        first_ref[half, start + TOK : start + 2 * TOK, :] = tile(EXPERTS + to)
        second_ref[half, :TOK, :] = tile(2 * EXPERTS + to)
        second_ref[half, TOK:, :] = jnp.where(low, left[:128], right[128:]).astype(bf16)


def build(tokens, routes):
    return pl.pallas_call(
        build_kernel,
        grid=(EXPERTS // 2,),
        in_specs=[
            pl.BlockSpec((TOK, tokens.shape[1]), lambda i: (0, 0)),
            pl.BlockSpec((2, TOK), lambda i: (0, 0)),
        ],
        out_specs=[
            pl.BlockSpec((2, FIRST_ROWS, 128), lambda i: (i, 0, 0)),
            pl.BlockSpec((2, SECOND_ROWS, 128), lambda i: (i, 0, 0)),
        ],
        out_shape=[
            pltpu.HBM((EXPERTS, FIRST_ROWS, 128), bf16),
            pltpu.HBM((EXPERTS, SECOND_ROWS, 128), bf16),
        ],
        scratch_shapes=[pltpu.VMEM((SLAB_ROWS, 128), bf16)],
        compiler_params=pltpu.CompilerParams(vmem_limit_bytes=24 * MIB),
        name="build",
    )(pltpu.with_memory_space_constraint(tokens, pltpu.HBM), routes)


def places_of(routes_rows):
    rows = routes_rows.astype(f32)
    one = jnp.concatenate([rows[0:1], rows[1:2]], axis=1)
    two = jnp.concatenate([rows[2:3], rows[3:4]], axis=1)
    expert = lax.broadcasted_iota(i32, (EXPERTS, TOK), 0).astype(f32)
    member = jnp.where((one == expert) | (two == expert), 1.0, 0.0)
    before = lax.broadcasted_iota(i32, (TOK, TOK), 0) < lax.broadcasted_iota(i32, (TOK, TOK), 1)
    earlier = jnp.dot(
        member.astype(bf16), jnp.where(before, 1.0, 0.0).astype(bf16), preferred_element_type=f32
    )
    return jnp.where(member > 0, earlier, -1.0)


def fill_pick(places, pick_ref, flip):
    slot = lax.broadcasted_iota(i32, (CAP, TOK), 0).astype(f32)
    for e in range(EXPERTS):
        hit = jnp.broadcast_to(places[e : e + 1, :], (CAP, TOK)) == slot
        to = (e ^ flip) * CAP
        pick_ref[to : to + CAP, :] = jnp.where(hit, 1.0, 0.0).astype(bf16)


def split_rows(here_ref, part_ref, keep_ref, send_ref, store):
    x, core = here_ref[0], here_ref[1]
    for step in range(4):
        owner = lax.rem(x + step, 4) * 2
        store(keep_ref, step, part_ref[owner + core])
        store(send_ref, step, part_ref[owner + 1 - core])


def note_largest(top_ref, product):
    largest = jnp.max(jnp.abs(product).reshape(-1, 8, product.shape[1]), axis=0)
    top_ref[...] = jnp.maximum(top_ref[...], jnp.maximum(largest[:, :128], largest[:, 128:]))


def slab_in_slots(pair, blocks, picks, slab):
    low = lax.broadcasted_iota(i32, (512, 128), 1) < CAP
    lanes = pl.ds(pl.multiple_of(pair * 128, 128), 128)
    rows = [jnp.concatenate([block[:512, :], block[512:SLAB_ROWS, :]], axis=1) for block in blocks]
    for quarter in range(4):
        got = [
            lax.dot_general(
                rows[source],
                picks[source][quarter * 256 : (quarter + 1) * 256, :],
                (((1,), (1,)), ((), ())),
                preferred_element_type=f32,
            ).astype(bf16)
            for source in range(2)
        ]
        for half in range(2):
            m = 2 * quarter + half
            a, b = (g[:, half * 128 : (half + 1) * 128] for g in got)
            slab[2 * m, :, lanes] = jnp.where(low, a, b)
            slab[2 * m + 1, :, lanes] = jnp.where(low, b, a)


def columns_in_slots(pair, cols, picks, held):
    for quarter in range(4):
        got = [
            jnp.dot(
                picks[source][quarter * 256 : (quarter + 1) * 256, :],
                cols[source],
                preferred_element_type=f32,
            ).astype(bf16)
            for source in range(2)
        ]
        for source in range(2):
            for block in range(4):
                e = (4 * quarter + block) ^ source
                offset = CAP * ((e + source) % 2)
                held[e, pl.ds(pl.multiple_of(pair * 128 + offset, CAP), CAP), :] = got[source][
                    block * CAP : (block + 1) * CAP
                ]


def slab_copy(slab, out_ref, sems, pair):
    lanes = pl.ds(pl.multiple_of(pair * 128, 128), 128)
    return pltpu.make_async_copy(slab.at[:, :, lanes], out_ref.at[pair], sems.at[pair])


def finish_notes(top_ref, counts):
    largest = jnp.broadcast_to(jnp.max(top_ref[...], keepdims=True), top_ref.shape)
    top_ref[...] = jnp.where(lax.broadcasted_iota(i32, top_ref.shape, 0) == 0, largest, counts)


def count_tokens(routes_rows):
    rows = routes_rows.astype(f32)
    expert = lax.broadcasted_iota(i32, (128, 128), 0).astype(f32)
    named = sum(jnp.where(rows[k : k + 1] == expert, 1.0, 0.0) for k in range(4))
    return lax.dot_general(
        jnp.ones((8, 128), bf16),
        named.astype(bf16),
        (((1,), (1,)), ((), ())),
        preferred_element_type=f32,
    )


def product0_kernel(
    here_ref, in_ref, keep_ref, send_ref, top_ref, slab_ref, places_ref, pick0, pick1, held, slab, sems, part, counts
):
    step = pl.program_id(0)

    @pl.when(step == 0)
    def _():
        top_ref[...] = jnp.zeros_like(top_ref)
        counts[...] = jnp.zeros_like(counts)

    @pl.when(step < 8)
    def _():
        blocks = [in_ref.at[source] for source in range(2)]
        start = SLAB_ROWS + ROUTE_ROWS
        cols = [
            jnp.concatenate(
                [block[start : start + TOK, :], block[start + TOK : start + 2 * TOK, :]], axis=1
            )
            for block in blocks
        ]
        picks = (pick0, pick1)
        for source in range(2):
            routes_rows = blocks[source][SLAB_ROWS : SLAB_ROWS + ROUTE_ROWS, :]
            counts[...] += count_tokens(routes_rows)
            places = places_of(routes_rows)
            places_ref[source] = places
            fill_pick(places, picks[source], source)
        slab_in_slots(step, blocks, picks, slab)
        slab_copy(slab, slab_ref, sems, step).start()
        columns_in_slots(step, cols, picks, held)

    @pl.when(step >= 8)
    def _():
        products = [
            jnp.dot(slab[e], held[e], preferred_element_type=f32)
            for e in (2 * (step - 8), 2 * (step - 8) + 1)
        ]
        for k in range(2):
            note_largest(top_ref, products[k])
            for tile in range(2):
                rows = slice(tile * 64, (tile + 1) * 64)
                part[k, :, rows, :] = products[k][:, tile * 128 : (tile + 1) * 128].reshape(8, 64, 128)
        for k in range(2):

            def store(ref, at, value):
                ref[at, k * 128 : (k + 1) * 128] = value

            split_rows(here_ref, part.at[k], keep_ref, send_ref, store)

    @pl.when(step == 15)
    def _():
        finish_notes(top_ref, counts[...])
        for pair in range(8):
            slab_copy(slab, slab_ref, sems, pair).wait()


PICKS = [pltpu.VMEM((1024, TOK), bf16)] * 2
HELD = pltpu.VMEM((EXPERTS, 1024, 256), bf16)


def early(i, here):
    return (jnp.minimum(i, 7), 0, 0)


def product0(here, first):
    rows = pl.BlockSpec((4, 256, 128), lambda i, here: (0, jnp.maximum(i - 8, 0), 0))
    return pl.pallas_call(
        product0_kernel,
        grid_spec=pltpu.PrefetchScalarGridSpec(
            num_scalar_prefetch=1,
            grid=(16,),
            in_specs=[pl.BlockSpec((2, FIRST_ROWS, 128), early)],
            out_specs=[
                rows,
                rows,
                pl.BlockSpec((8, 128), lambda i, here: (0, 0)),
                pl.BlockSpec(memory_space=pl.ANY),
                pl.BlockSpec((2, EXPERTS, TOK), early),
            ],
            scratch_shapes=[
                *PICKS,
                HELD,
                pltpu.VMEM((EXPERTS, 512, 1024), bf16),
                pltpu.SemaphoreType.DMA((8,)),
                pltpu.VMEM((2, 8, 128, 128), f32),
                pltpu.VMEM((8, 128), f32),
            ],
        ),
        out_shape=[pltpu.HBM((4, EXPERTS * 128 + EXTRA, 128), f32)] * 2
        + [
            jax.ShapeDtypeStruct((8, 128), f32),
            pltpu.HBM((8, EXPERTS, 512, 128), bf16),
            jax.ShapeDtypeStruct((EXPERTS, EXPERTS, TOK), f32),
        ],
        compiler_params=pltpu.CompilerParams(vmem_limit_bytes=40 * MIB),
        cost_estimate=pl.CostEstimate(flops=11 * 10**9, bytes_accessed=16 * 10**6, transcendentals=0),
        name="product0",
    )(here, pltpu.with_memory_space_constraint(first, pltpu.HBM))


def product1_kernel(
    here_ref, places_ref, cols_ref, slab_ref, keep_ref, send_ref, top_ref, pick0, pick1, held, part, slab, sems
):
    step = pl.program_id(0)

    def fetch(pair):
        return pltpu.make_async_copy(
            slab_ref.at[:, pl.ds(2 * pair, 2)], slab.at[pair], sems.at[pair]
        )

    @pl.when(step == 0)
    def _():
        top_ref[...] = jnp.zeros_like(top_ref)
        for pair in range(8):
            fetch(pair).start()

    @pl.when(step < 8)
    def _():
        picks = (pick0, pick1)
        cols = []
        for source in range(2):
            fill_pick(places_ref[source], picks[source], source)
            last = cols_ref[source, TOK:, :]
            turned = pltpu.roll(last.astype(f32), 64, 1).astype(bf16)
            last = jnp.concatenate([last, turned], axis=0)
            cols.append(jnp.concatenate([cols_ref[source, :TOK, :], last], axis=1))
        columns_in_slots(step, cols, picks, held)

    @pl.when(step >= 8)
    def _():
        fetch(step - 8).wait()
        products = [
            jnp.dot(
                jnp.concatenate([slab[step - 8, pair, k] for pair in range(8)], axis=1),
                held[2 * (step - 8) + k],
                preferred_element_type=f32,
            )
            for k in range(2)
        ]
        low = lax.broadcasted_iota(i32, (8, 32, 128), 2) < 64
        for k in range(2):
            note_largest(top_ref, products[k])
            part[k, :, :64, :] = products[k][:, :128].reshape(8, 64, 128)
            halves = products[k][:, 128:].reshape(8, 2, 32, 128)
            turned = pltpu.roll(products[k][:, 128:], 64, 1).reshape(8, 2, 32, 128)
            part[k, :, 64:, :] = jnp.where(low, halves[:, 0], turned[:, 1])
        for k in range(2):

            def store(ref, at, value):
                ref[at, k * 96 : (k + 1) * 96] = value

            split_rows(here_ref, part.at[k], keep_ref, send_ref, store)

    @pl.when(step == 15)
    def _():
        finish_notes(top_ref, 0.0)


def product1(here, places, second, slab):
    rows = pl.BlockSpec((4, 192, 128), lambda i, here: (0, jnp.maximum(i - 8, 0), 0))
    return pl.pallas_call(
        product1_kernel,
        grid_spec=pltpu.PrefetchScalarGridSpec(
            num_scalar_prefetch=1,
            grid=(16,),
            in_specs=[
                pl.BlockSpec((2, EXPERTS, TOK), early),
                pl.BlockSpec((2, SECOND_ROWS, 128), early),
                pl.BlockSpec(memory_space=pl.ANY),
            ],
            out_specs=[rows, rows, pl.BlockSpec((8, 128), lambda i, here: (0, 0))],
            scratch_shapes=[
                *PICKS,
                HELD,
                pltpu.VMEM((2, 8, 96, 128), f32),
                pltpu.VMEM((8, 8, 2, 512, 128), bf16),
                pltpu.SemaphoreType.DMA((8,)),
            ],
        ),
        out_shape=[pltpu.HBM((4, EXPERTS * 96 + EXTRA, 128), f32)] * 2
        + [jax.ShapeDtypeStruct((8, 128), f32)],
        compiler_params=pltpu.CompilerParams(vmem_limit_bytes=40 * MIB),
        cost_estimate=pl.CostEstimate(flops=11 * 10**9, bytes_accessed=16 * 10**6, transcendentals=0),
        name="product1",
    )(here, places, second, slab)


def over_core(send, top):
    return lax.ppermute(send, "core", SWAP), top + lax.ppermute(top, "core", SWAP)


def sum_over_core(keep, other, top):
    top, counts = top[:1], top[1:2]
    exponent = jnp.clip(jnp.floor(jnp.log2(32000.0 / jnp.maximum(top, 1e-30))), -100.0, 100.0)
    exponent, factor = lax.optimization_barrier((exponent, jnp.exp2(exponent)))
    rows = keep.shape[1] - EXTRA
    row = lax.broadcasted_iota(i32, keep.shape[1:], 0)
    more = jnp.where(row == rows + 1, counts, exponent)
    others = [
        jnp.where(row < rows, (keep[i] + other[i]) * factor, more).astype(f16) for i in (1, 2, 3)
    ]
    return (keep[0], other[0], exponent, counts), others


def sum_over_x(own, others):
    rows = own[0].shape[0] - EXTRA
    exponents = [value[rows : rows + 1].astype(f32) for value in others]
    one, two, three = (
        value.astype(f32) * jnp.exp2(-exponent) for value, exponent in zip(others, exponents)
    )
    least = functools.reduce(jnp.minimum, exponents, own[2]) - 2.0
    total = (own[0] + own[1] + two) + (one + three)
    counts = own[3] + sum(value[rows + 1 : rows + 2].astype(f32) for value in others)
    return (total * jnp.exp2(least))[:rows].astype(f16), least, counts


def over_x(others):
    return [lax.ppermute(value, "x", pairs) for value, pairs in zip(others, (UP, OPPOSITE, DOWN))]


def order_kernel(scale_ref, a_ref, b_ref, out_ref):
    scale = scale_ref[0]
    for i in range(EXPERTS):
        out_ref[:, i * 128 : (i + 1) * 128] = a_ref[i, :64, :] * scale
        out_ref[:, (16 + i) * 128 : (17 + i) * 128] = a_ref[i, 64:, :] * scale
        out_ref[:, (32 + i) * 128 : (33 + i) * 128] = b_ref[i, :64, :] * scale
    low = lax.broadcasted_iota(i32, (32, 128), 1) < 64
    for t in range(8):
        left, right = b_ref[2 * t, 64:, :], b_ref[2 * t + 1, 64:, :]
        columns = slice((48 + t) * 128, (49 + t) * 128)
        out_ref[:32, columns] = jnp.where(low, left, pltpu.roll(right, 64, 1)) * scale
        out_ref[32:, columns] = jnp.where(low, pltpu.roll(left, 64, 1), right) * scale


def put_in_order(scale, a, b):
    smem, vmem = pl.BlockSpec(memory_space=pltpu.SMEM), pl.BlockSpec(memory_space=pltpu.VMEM)
    return pl.pallas_call(
        order_kernel,
        in_specs=[smem, vmem, vmem],
        out_specs=vmem,
        out_shape=jax.ShapeDtypeStruct((64, 7168), f32),
        compiler_params=pltpu.CompilerParams(vmem_limit_bytes=16 * MIB),
        name="put_in_order",
    )(scale, a, b)


def columns_kernel(
    block_ref, levels_ref, pivots_ref, diag_ref, snapped_ref, errors_ref, now, out, err, upper_ref, turned_ref
):
    block = block_ref[...].astype(f32).T
    now[...] = block
    largest = jnp.max(jnp.abs(block), axis=0, keepdims=True)
    spacing = (largest + 1e-05) / levels_ref[...].astype(f32)
    per_turn = 1.0 / spacing
    reach = 0.9 * spacing / (2.0 * math.pi)
    lane = lax.broadcasted_iota(i32, (8, BLOCK), 1)
    row, column = (lax.broadcasted_iota(i32, (BLOCK, BLOCK), d) for d in range(2))
    upper = jnp.where(column > row, diag_ref[...], 0.0)
    upper_ref[...] = upper
    turned_ref[...] = upper.T

    def group(b, carry):
        at = pl.multiple_of(b * 8, 8)
        tile = now[pl.ds(at, 8), :]
        turned = turned_ref[pl.ds(at, 8), :]
        near = [
            jnp.sum(jnp.where(lane == at + i, turned, 0.0), axis=1, keepdims=True) for i in range(8)
        ]
        snapped, errors = [], []
        for i in range(8):
            values = tile[i : i + 1, :]
            moved = values - reach * sine_turns(values * per_turn)
            error = (values - moved) * pivots_ref[at + i]
            tile = tile - near[i] * error
            snapped.append(moved)
            errors.append(error)
        errors = jnp.concatenate(errors, axis=0)
        out[pl.ds(at, 8), :] = jnp.concatenate(snapped, axis=0)
        err[pl.ds(at, 8), :] = errors
        now[...] -= lax.dot_general(
            upper_ref[pl.ds(at, 8), :],
            errors,
            (((0,), (0,)), ((), ())),
            precision=lax.Precision.HIGHEST,
            preferred_element_type=f32,
        )
        return carry

    lax.fori_loop(0, BLOCK // 8, group, 0)
    snapped_ref[...] = out[...].T
    errors_ref[...] = err[...].T


def block_update(rows, levels, pivots, panel_diag):
    whole = lambda *shape: pl.BlockSpec(shape, lambda i: (0,) * len(shape))
    count = rows.shape[0]
    return pl.pallas_call(
        columns_kernel,
        grid=(1,),
        in_specs=[
            whole(count, BLOCK),
            whole(1, count),
            pl.BlockSpec(memory_space=pltpu.SMEM),
            whole(BLOCK, BLOCK),
        ],
        out_specs=[whole(count, BLOCK)] * 2,
        out_shape=[jax.ShapeDtypeStruct((count, BLOCK), f32)] * 2,
        scratch_shapes=[pltpu.VMEM((BLOCK, count), f32)] * 3 + [pltpu.VMEM((BLOCK, BLOCK), f32)] * 2,
        compiler_params=pltpu.CompilerParams(vmem_limit_bytes=16 * MIB),
        cost_estimate=pl.CostEstimate(flops=10**9, bytes_accessed=2 * 10**6, transcendentals=0),
        name="block_update",
    )(pltpu.with_memory_space_constraint(rows, pltpu.HBM), levels, 1.0 / pivots, panel_diag)


def ahead_over_x(mine):
    return [mine] + [lax.ppermute(mine, "x", pairs) for pairs in (DOWN, OPPOSITE, UP)]


def later_kernel(here_ref, errors_ref, own_ref, other_ref, *refs):
    *weight_refs, out_ref, panel, parts = refs
    i = pl.program_id(0)
    wide = panel.shape[0] // 8
    count = errors_ref.shape[0]

    @pl.when(i == 0)
    def _():
        x, core = here_ref[0], here_ref[1]
        for at in range(4):
            ahead = lax.rem(at + 4 - x, 4)
            mine = pl.multiple_of((2 * at + core) * wide, 16)
            theirs = pl.multiple_of((2 * at + 1 - core) * wide, 16)
            panel[pl.ds(mine, wide), :] = own_ref[ahead, :wide, :]
            panel[pl.ds(theirs, wide), :] = other_ref[ahead, :wide, :]
        errors = errors_ref[...]
        for k in range(3):
            part = errors.astype(bf16)
            errors = errors - part.astype(f32)
            parts[k * count : (k + 1) * count, :] = part

    got = lax.dot_general(
        parts[...],
        panel[pl.ds(pl.multiple_of(i * 640, 128), 640), :],
        (((1,), (1,)), ((), ())),
        preferred_element_type=f32,
    )
    total = (got[:count] + got[count : 2 * count]) + got[2 * count :]
    for k, ref in enumerate(weight_refs):
        out_ref[:, k * 128 : (k + 1) * 128] = ref[...].astype(f32) - total[:, k * 128 : (k + 1) * 128]


def later_columns(here, rows, errors, own, other):
    count, later = rows.shape[0], rows.shape[1] - BLOCK
    columns = [
        pl.BlockSpec((count, 128), functools.partial(lambda k, i, here: (0, 5 * i + k), k))
        for k in range(1, 6)
    ]
    whole = lambda a: pl.BlockSpec(a.shape, lambda i, here: (0,) * a.ndim)
    return pl.pallas_call(
        later_kernel,
        grid_spec=pltpu.PrefetchScalarGridSpec(
            num_scalar_prefetch=1,
            grid=(later // 640,),
            in_specs=[whole(errors), whole(own), whole(other)] + columns,
            out_specs=pl.BlockSpec((count, 640), lambda i, here: (0, i)),
            scratch_shapes=[pltpu.VMEM((later, BLOCK), bf16), pltpu.VMEM((3 * count, BLOCK), bf16)],
        ),
        out_shape=pltpu.HBM((count, later), f32),
        compiler_params=pltpu.CompilerParams(vmem_limit_bytes=24 * MIB),
        cost_estimate=pl.CostEstimate(flops=15 * 10**8, bytes_accessed=13 * 10**6, transcendentals=0),
        name="later_columns",
    )(here, errors, own, other, *[pltpu.with_memory_space_constraint(rows, pltpu.HBM)] * 5)


def on_device(tokens, routes, weight, levels, pivots, panel_diag, panel_rest):
    x, core = lax.axis_index("x"), lax.axis_index("core")
    place = lax.axis_index("z") * 4 + lax.axis_index("y")
    exchange = functools.partial(
        lax.all_to_all, axis_name=PLANE, split_axis=0, concat_axis=0, tiled=True
    )
    here = jnp.stack([x, core]).astype(i32)

    first, second = build(tokens, routes.T)
    first, here, place, pivots = lax.optimization_barrier((first, here, place, pivots))
    first = exchange(first)
    first, second, weight, levels, panel_diag, panel_rest, pivots = lax.optimization_barrier(
        (first, second, weight, levels, panel_diag, panel_rest, pivots)
    )
    second = exchange(second)
    keep, send, top, slab, places = product0(here, first)
    keep, send, top, second, slab, places, panel_rest = lax.optimization_barrier(
        (keep, send, top, second, slab, places, panel_rest)
    )
    panel = ahead_over_x(panel_rest[0].T.astype(bf16))
    own, others = sum_over_core(keep, *over_core(send, top))
    places, second, slab, others = lax.optimization_barrier((places, second, slab, others))
    others = over_x(others)
    keep, send, top = product1(here, places, second, slab)
    keep, send, top, others, panel, weight = lax.optimization_barrier(
        (keep, send, top, others, panel, weight)
    )
    panel = jnp.stack(panel)
    far_own, far_others = own, others
    own, others = sum_over_core(keep, *over_core(send, top))

    others, rows, panel, far_others = lax.optimization_barrier((others, weight[0], panel, far_others))
    others = over_x(others)
    total, least, counts = sum_over_x(far_own, far_others)
    snapped, errors = block_update(rows, levels, pivots[0], panel_diag[0])
    other_panel = lax.ppermute(panel, "core", SWAP)
    others, errors, other_panel, total, least = lax.optimization_barrier(
        (others, errors, other_panel, total, least)
    )
    tail, last, _ = sum_over_x(own, others)
    sent = [total.reshape(EXPERTS, 128, 128), tail.reshape(EXPERTS, 96, 128)]
    first_rows = lax.broadcasted_iota(i32, (EXPERTS, 16, 128), 1) < 8
    sent.append(jnp.where(first_rows, least, last).astype(f16))
    sums = exchange(jnp.concatenate(sent, axis=1))

    remainder = later_columns(here, rows, errors, panel, other_panel)

    own_count = lax.dynamic_index_in_dim(counts[0], place, 0, keepdims=True)
    total = sums[:, :128].astype(f32) * jnp.exp2(-sums[:, 224:225].astype(f32))
    tail = sums[:, 128:224].astype(f32) * jnp.exp2(-sums[:, 232:233].astype(f32))
    hessian = put_in_order(2.0 / own_count, total, tail)
    return hessian[None], snapped[None], remainder[None]


def solution(mesh):
    devices = mesh.devices
    fine = Mesh(devices.reshape(4, 2, 4, 4), ("x", "core", "z", "y"))
    dp, every = ("x", "core"), ("x", "core", "z", "y")
    return jax.shard_map(
        on_device,
        mesh=fine,
        in_specs=(
            P(every, None),
            P(every, None),
            P(PLANE, dp, None),
            P(PLANE, dp),
            P(PLANE, None),
            P(PLANE, None, None),
            P(PLANE, None, dp),
        ),
        out_specs=(P(PLANE, dp, None),) * 3,
        check_vma=False,
    )
```

```python
import functools
import math

import jax
import jax.numpy as jnp
import numpy as np
from jax import lax
from jax.experimental import pallas as pl
from jax.experimental.pallas import tpu as pltpu
from jax.sharding import Mesh
from jax.sharding import PartitionSpec as P

BLOCK = 128
PLANE = ("z", "y")
EXPERTS = 16
TOK = 256
CAP = 64
MIB = 1024 * 1024
UP = [(i, (i + 1) % 4) for i in range(4)]
DOWN = [(i, (i - 1) % 4) for i in range(4)]
OPPOSITE = [(i, (i + 2) % 4) for i in range(4)]
SWAP = [(0, 1), (1, 0)]
bf16, f16, f32, i32 = jnp.bfloat16, jnp.float16, jnp.float32, jnp.int32
SLAB_ROWS, ROUTE_ROWS = 4 * TOK, 16
FIRST_ROWS = SLAB_ROWS + ROUTE_ROWS + 2 * TOK
SECOND_ROWS = TOK + TOK // 2
EXTRA = 16


def sine_coefficients():
    nodes = 0.5 * np.cos(np.pi * (np.arange(400) + 0.5) / 800)
    powers = np.stack([nodes ** (2 * k + 1) for k in range(8)], 1)
    scale = 1.0 / np.abs(powers).max(0)
    fit = np.linalg.lstsq(powers * scale, np.sin(2 * np.pi * nodes), rcond=None)[0]
    return [float(c) for c in fit * scale]


SINE = sine_coefficients()


def sine_turns(turns):
    r = turns - jnp.round(turns)
    s = r * r
    total = jnp.full_like(r, SINE[-1])
    for c in SINE[-2::-1]:
        total = total * s + c
    return total * r


def build_kernel(tokens_ref, routes_ref, first_ref, second_ref, slab):
    i = pl.program_id(0)
    routes = routes_ref[...].astype(f32)
    halves = [routes[k : k + 1, at : at + 128] for k in range(2) for at in (0, 128)]
    routes_rows = jnp.concatenate([*halves, jnp.zeros((ROUTE_ROWS - 4, 128), f32)], axis=0).astype(bf16)

    @pl.when(i == 0)
    def _():
        for tile in range(4):
            turned = tokens_ref[:, tile * 128 : (tile + 1) * 128].astype(f32).T.astype(bf16)
            slab[tile * 128 : (tile + 1) * 128, :] = turned[:, :128]
            slab[512 + tile * 128 : 512 + (tile + 1) * 128, :] = turned[:, 128:]

    def tile(k):
        return tokens_ref[:, pl.ds(pl.multiple_of(k * 128, 128), 128)]

    low = lax.broadcasted_iota(i32, (128, 128), 1) < 64
    last = tile(3 * EXPERTS + i).astype(f32)
    turned = pltpu.roll(last, 64, 1)
    for half, (left, right) in enumerate(((last, turned), (turned, last))):
        to = 2 * i + half
        first_ref[half, :SLAB_ROWS, :] = slab[...]
        first_ref[half, SLAB_ROWS : SLAB_ROWS + ROUTE_ROWS, :] = routes_rows
        start = SLAB_ROWS + ROUTE_ROWS
        first_ref[half, start : start + TOK, :] = tile(to)
        first_ref[half, start + TOK : start + 2 * TOK, :] = tile(EXPERTS + to)
        second_ref[half, :TOK, :] = tile(2 * EXPERTS + to)
        second_ref[half, TOK:, :] = jnp.where(low, left[:128], right[128:]).astype(bf16)


def build(tokens, routes):
    return pl.pallas_call(
        build_kernel,
        grid=(EXPERTS // 2,),
        in_specs=[
            pl.BlockSpec((TOK, tokens.shape[1]), lambda i: (0, 0)),
            pl.BlockSpec((2, TOK), lambda i: (0, 0)),
        ],
        out_specs=[
            pl.BlockSpec((2, FIRST_ROWS, 128), lambda i: (i, 0, 0)),
            pl.BlockSpec((2, SECOND_ROWS, 128), lambda i: (i, 0, 0)),
        ],
        out_shape=[
            pltpu.HBM((EXPERTS, FIRST_ROWS, 128), bf16),
            pltpu.HBM((EXPERTS, SECOND_ROWS, 128), bf16),
        ],
        scratch_shapes=[pltpu.VMEM((SLAB_ROWS, 128), bf16)],
        compiler_params=pltpu.CompilerParams(vmem_limit_bytes=24 * MIB),
        name="build",
    )(pltpu.with_memory_space_constraint(tokens, pltpu.HBM), routes)


def places_of(routes_rows):
    rows = routes_rows.astype(f32)
    one = jnp.concatenate([rows[0:1], rows[1:2]], axis=1)
    two = jnp.concatenate([rows[2:3], rows[3:4]], axis=1)
    expert = lax.broadcasted_iota(i32, (EXPERTS, TOK), 0).astype(f32)
    member = jnp.where((one == expert) | (two == expert), 1.0, 0.0)
    before = lax.broadcasted_iota(i32, (TOK, TOK), 0) < lax.broadcasted_iota(i32, (TOK, TOK), 1)
    earlier = jnp.dot(
        member.astype(bf16), jnp.where(before, 1.0, 0.0).astype(bf16), preferred_element_type=f32
    )
    return jnp.where(member > 0, earlier, -1.0)


def fill_pick(places, pick_ref, flip):
    slot = lax.broadcasted_iota(i32, (CAP, TOK), 0).astype(f32)
    for e in range(EXPERTS):
        hit = jnp.broadcast_to(places[e : e + 1, :], (CAP, TOK)) == slot
        to = (e ^ flip) * CAP
        pick_ref[to : to + CAP, :] = jnp.where(hit, 1.0, 0.0).astype(bf16)


def split_rows(here_ref, part_ref, keep_ref, send_ref, store):
    x, core = here_ref[0], here_ref[1]
    for step in range(4):
        owner = lax.rem(x + step, 4) * 2
        store(keep_ref, step, part_ref[owner + core])
        store(send_ref, step, part_ref[owner + 1 - core])


def note_largest(top_ref, product):
    largest = jnp.max(jnp.abs(product).reshape(-1, 8, product.shape[1]), axis=0)
    top_ref[...] = jnp.maximum(top_ref[...], jnp.maximum(largest[:, :128], largest[:, 128:]))


def slab_in_slots(pair, blocks, picks, slab):
    low = lax.broadcasted_iota(i32, (512, 128), 1) < CAP
    lanes = pl.ds(pl.multiple_of(pair * 128, 128), 128)
    rows = [jnp.concatenate([block[:512, :], block[512:SLAB_ROWS, :]], axis=1) for block in blocks]
    for quarter in range(4):
        got = [
            lax.dot_general(
                rows[source],
                picks[source][quarter * 256 : (quarter + 1) * 256, :],
                (((1,), (1,)), ((), ())),
                preferred_element_type=f32,
            ).astype(bf16)
            for source in range(2)
        ]
        for half in range(2):
            m = 2 * quarter + half
            a, b = (g[:, half * 128 : (half + 1) * 128] for g in got)
            slab[2 * m, :, lanes] = jnp.where(low, a, b)
            slab[2 * m + 1, :, lanes] = jnp.where(low, b, a)


def columns_in_slots(pair, cols, picks, held):
    for quarter in range(4):
        got = [
            jnp.dot(
                picks[source][quarter * 256 : (quarter + 1) * 256, :],
                cols[source],
                preferred_element_type=f32,
            ).astype(bf16)
            for source in range(2)
        ]
        for source in range(2):
            for block in range(4):
                e = (4 * quarter + block) ^ source
                offset = CAP * ((e + source) % 2)
                held[e, pl.ds(pl.multiple_of(pair * 128 + offset, CAP), CAP), :] = got[source][
                    block * CAP : (block + 1) * CAP
                ]


def slab_copy(slab, out_ref, sems, pair):
    lanes = pl.ds(pl.multiple_of(pair * 128, 128), 128)
    return pltpu.make_async_copy(slab.at[:, :, lanes], out_ref.at[pair], sems.at[pair])


def finish_notes(top_ref, counts):
    largest = jnp.broadcast_to(jnp.max(top_ref[...], keepdims=True), top_ref.shape)
    top_ref[...] = jnp.where(lax.broadcasted_iota(i32, top_ref.shape, 0) == 0, largest, counts)


def count_tokens(routes_rows):
    rows = routes_rows.astype(f32)
    expert = lax.broadcasted_iota(i32, (128, 128), 0).astype(f32)
    named = sum(jnp.where(rows[k : k + 1] == expert, 1.0, 0.0) for k in range(4))
    return lax.dot_general(
        jnp.ones((8, 128), bf16),
        named.astype(bf16),
        (((1,), (1,)), ((), ())),
        preferred_element_type=f32,
    )


def product0_kernel(
    here_ref, in_ref, keep_ref, send_ref, top_ref, slab_ref, places_ref, pick0, pick1, held, slab, sems, part, counts
):
    step = pl.program_id(0)

    @pl.when(step == 0)
    def _():
        top_ref[...] = jnp.zeros_like(top_ref)
        counts[...] = jnp.zeros_like(counts)

    @pl.when(step < 8)
    def _():
        blocks = [in_ref.at[source] for source in range(2)]
        start = SLAB_ROWS + ROUTE_ROWS
        cols = [
            jnp.concatenate(
                [block[start : start + TOK, :], block[start + TOK : start + 2 * TOK, :]], axis=1
            )
            for block in blocks
        ]
        picks = (pick0, pick1)
        for source in range(2):
            routes_rows = blocks[source][SLAB_ROWS : SLAB_ROWS + ROUTE_ROWS, :]
            counts[...] += count_tokens(routes_rows)
            places = places_of(routes_rows)
            places_ref[source] = places
            fill_pick(places, picks[source], source)
        slab_in_slots(step, blocks, picks, slab)
        slab_copy(slab, slab_ref, sems, step).start()
        columns_in_slots(step, cols, picks, held)

    @pl.when(step >= 8)
    def _():
        products = [
            jnp.dot(slab[e], held[e], preferred_element_type=f32)
            for e in (2 * (step - 8), 2 * (step - 8) + 1)
        ]
        for k in range(2):
            note_largest(top_ref, products[k])
            for tile in range(2):
                rows = slice(tile * 64, (tile + 1) * 64)
                part[k, :, rows, :] = products[k][:, tile * 128 : (tile + 1) * 128].reshape(8, 64, 128)
        for k in range(2):

            def store(ref, at, value):
                ref[at, k * 128 : (k + 1) * 128] = value

            split_rows(here_ref, part.at[k], keep_ref, send_ref, store)

    @pl.when(step == 15)
    def _():
        finish_notes(top_ref, counts[...])
        for pair in range(8):
            slab_copy(slab, slab_ref, sems, pair).wait()


PICKS = [pltpu.VMEM((1024, TOK), bf16)] * 2
HELD = pltpu.VMEM((EXPERTS, 1024, 256), bf16)


def early(i, here):
    return (jnp.minimum(i, 7), 0, 0)


def product0(here, first):
    rows = pl.BlockSpec((4, 256, 128), lambda i, here: (0, jnp.maximum(i - 8, 0), 0))
    return pl.pallas_call(
        product0_kernel,
        grid_spec=pltpu.PrefetchScalarGridSpec(
            num_scalar_prefetch=1,
            grid=(16,),
            in_specs=[pl.BlockSpec((2, FIRST_ROWS, 128), early)],
            out_specs=[
                rows,
                rows,
                pl.BlockSpec((8, 128), lambda i, here: (0, 0)),
                pl.BlockSpec(memory_space=pl.ANY),
                pl.BlockSpec((2, EXPERTS, TOK), early),
            ],
            scratch_shapes=[
                *PICKS,
                HELD,
                pltpu.VMEM((EXPERTS, 512, 1024), bf16),
                pltpu.SemaphoreType.DMA((8,)),
                pltpu.VMEM((2, 8, 128, 128), f32),
                pltpu.VMEM((8, 128), f32),
            ],
        ),
        out_shape=[pltpu.HBM((4, EXPERTS * 128 + EXTRA, 128), f32)] * 2
        + [
            jax.ShapeDtypeStruct((8, 128), f32),
            pltpu.HBM((8, EXPERTS, 512, 128), bf16),
            jax.ShapeDtypeStruct((EXPERTS, EXPERTS, TOK), f32),
        ],
        compiler_params=pltpu.CompilerParams(vmem_limit_bytes=40 * MIB),
        cost_estimate=pl.CostEstimate(flops=11 * 10**9, bytes_accessed=16 * 10**6, transcendentals=0),
        name="product0",
    )(here, pltpu.with_memory_space_constraint(first, pltpu.HBM))


def product1_kernel(
    here_ref, places_ref, cols_ref, slab_ref, keep_ref, send_ref, top_ref, pick0, pick1, held, part, slab, sems
):
    step = pl.program_id(0)

    def fetch(pair):
        return pltpu.make_async_copy(
            slab_ref.at[:, pl.ds(2 * pair, 2)], slab.at[pair], sems.at[pair]
        )

    @pl.when(step == 0)
    def _():
        top_ref[...] = jnp.zeros_like(top_ref)
        for pair in range(8):
            fetch(pair).start()

    @pl.when(step < 8)
    def _():
        picks = (pick0, pick1)
        cols = []
        for source in range(2):
            fill_pick(places_ref[source], picks[source], source)
            last = cols_ref[source, TOK:, :]
            turned = pltpu.roll(last.astype(f32), 64, 1).astype(bf16)
            last = jnp.concatenate([last, turned], axis=0)
            cols.append(jnp.concatenate([cols_ref[source, :TOK, :], last], axis=1))
        columns_in_slots(step, cols, picks, held)

    @pl.when(step >= 8)
    def _():
        fetch(step - 8).wait()
        products = [
            jnp.dot(
                jnp.concatenate([slab[step - 8, pair, k] for pair in range(8)], axis=1),
                held[2 * (step - 8) + k],
                preferred_element_type=f32,
            )
            for k in range(2)
        ]
        low = lax.broadcasted_iota(i32, (8, 32, 128), 2) < 64
        for k in range(2):
            note_largest(top_ref, products[k])
            part[k, :, :64, :] = products[k][:, :128].reshape(8, 64, 128)
            halves = products[k][:, 128:].reshape(8, 2, 32, 128)
            turned = pltpu.roll(products[k][:, 128:], 64, 1).reshape(8, 2, 32, 128)
            part[k, :, 64:, :] = jnp.where(low, halves[:, 0], turned[:, 1])
        for k in range(2):

            def store(ref, at, value):
                ref[at, k * 96 : (k + 1) * 96] = value

            split_rows(here_ref, part.at[k], keep_ref, send_ref, store)

    @pl.when(step == 15)
    def _():
        finish_notes(top_ref, 0.0)


def product1(here, places, second, slab):
    rows = pl.BlockSpec((4, 192, 128), lambda i, here: (0, jnp.maximum(i - 8, 0), 0))
    return pl.pallas_call(
        product1_kernel,
        grid_spec=pltpu.PrefetchScalarGridSpec(
            num_scalar_prefetch=1,
            grid=(16,),
            in_specs=[
                pl.BlockSpec((2, EXPERTS, TOK), early),
                pl.BlockSpec((2, SECOND_ROWS, 128), early),
                pl.BlockSpec(memory_space=pl.ANY),
            ],
            out_specs=[rows, rows, pl.BlockSpec((8, 128), lambda i, here: (0, 0))],
            scratch_shapes=[
                *PICKS,
                HELD,
                pltpu.VMEM((2, 8, 96, 128), f32),
                pltpu.VMEM((8, 8, 2, 512, 128), bf16),
                pltpu.SemaphoreType.DMA((8,)),
            ],
        ),
        out_shape=[pltpu.HBM((4, EXPERTS * 96 + EXTRA, 128), f32)] * 2
        + [jax.ShapeDtypeStruct((8, 128), f32)],
        compiler_params=pltpu.CompilerParams(vmem_limit_bytes=40 * MIB),
        cost_estimate=pl.CostEstimate(flops=11 * 10**9, bytes_accessed=16 * 10**6, transcendentals=0),
        name="product1",
    )(here, places, second, slab)


def over_core(send, top):
    return lax.ppermute(send, "core", SWAP), top + lax.ppermute(top, "core", SWAP)


def sum_over_core(keep, other, top):
    top, counts = top[:1], top[1:2]
    exponent = jnp.clip(jnp.floor(jnp.log2(32000.0 / jnp.maximum(top, 1e-30))), -100.0, 100.0)
    exponent, factor = lax.optimization_barrier((exponent, jnp.exp2(exponent)))
    rows = keep.shape[1] - EXTRA
    row = lax.broadcasted_iota(i32, keep.shape[1:], 0)
    more = jnp.where(row == rows + 1, counts, exponent)
    others = [
        jnp.where(row < rows, (keep[i] + other[i]) * factor, more).astype(f16) for i in (1, 2, 3)
    ]
    return (keep[0], other[0], exponent, counts), others


def sum_over_x(own, others):
    rows = own[0].shape[0] - EXTRA
    exponents = [value[rows : rows + 1].astype(f32) for value in others]
    one, two, three = (
        value.astype(f32) * jnp.exp2(-exponent) for value, exponent in zip(others, exponents)
    )
    least = functools.reduce(jnp.minimum, exponents, own[2]) - 2.0
    total = (own[0] + own[1] + two) + (one + three)
    counts = own[3] + sum(value[rows + 1 : rows + 2].astype(f32) for value in others)
    return (total * jnp.exp2(least))[:rows].astype(f16), least, counts


def over_x(others):
    return [lax.ppermute(value, "x", pairs) for value, pairs in zip(others, (UP, OPPOSITE, DOWN))]


def order_kernel(scale_ref, a_ref, b_ref, out_ref):
    scale = scale_ref[0]
    for i in range(EXPERTS):
        out_ref[:, i * 128 : (i + 1) * 128] = a_ref[i, :64, :] * scale
        out_ref[:, (16 + i) * 128 : (17 + i) * 128] = a_ref[i, 64:, :] * scale
        out_ref[:, (32 + i) * 128 : (33 + i) * 128] = b_ref[i, :64, :] * scale
    low = lax.broadcasted_iota(i32, (32, 128), 1) < 64
    for t in range(8):
        left, right = b_ref[2 * t, 64:, :], b_ref[2 * t + 1, 64:, :]
        columns = slice((48 + t) * 128, (49 + t) * 128)
        out_ref[:32, columns] = jnp.where(low, left, pltpu.roll(right, 64, 1)) * scale
        out_ref[32:, columns] = jnp.where(low, pltpu.roll(left, 64, 1), right) * scale


def put_in_order(scale, a, b):
    smem, vmem = pl.BlockSpec(memory_space=pltpu.SMEM), pl.BlockSpec(memory_space=pltpu.VMEM)
    return pl.pallas_call(
        order_kernel,
        in_specs=[smem, vmem, vmem],
        out_specs=vmem,
        out_shape=jax.ShapeDtypeStruct((64, 7168), f32),
        compiler_params=pltpu.CompilerParams(vmem_limit_bytes=16 * MIB),
        name="put_in_order",
    )(scale, a, b)


def columns_kernel(
    block_ref, levels_ref, pivots_ref, diag_ref, snapped_ref, errors_ref, now, out, err, upper_ref, turned_ref
):
    block = block_ref[...].astype(f32).T
    now[...] = block
    largest = jnp.max(jnp.abs(block), axis=0, keepdims=True)
    spacing = (largest + 1e-05) / levels_ref[...].astype(f32)
    per_turn = 1.0 / spacing
    reach = 0.9 * spacing / (2.0 * math.pi)
    lane = lax.broadcasted_iota(i32, (8, BLOCK), 1)
    row, column = (lax.broadcasted_iota(i32, (BLOCK, BLOCK), d) for d in range(2))
    upper = jnp.where(column > row, diag_ref[...], 0.0)
    upper_ref[...] = upper
    turned_ref[...] = upper.T

    def group(b, carry):
        at = pl.multiple_of(b * 8, 8)
        tile = now[pl.ds(at, 8), :]
        turned = turned_ref[pl.ds(at, 8), :]
        near = [
            jnp.sum(jnp.where(lane == at + i, turned, 0.0), axis=1, keepdims=True) for i in range(8)
        ]
        snapped, errors = [], []
        for i in range(8):
            values = tile[i : i + 1, :]
            moved = values - reach * sine_turns(values * per_turn)
            error = (values - moved) * pivots_ref[at + i]
            tile = tile - near[i] * error
            snapped.append(moved)
            errors.append(error)
        errors = jnp.concatenate(errors, axis=0)
        out[pl.ds(at, 8), :] = jnp.concatenate(snapped, axis=0)
        err[pl.ds(at, 8), :] = errors
        now[...] -= lax.dot_general(
            upper_ref[pl.ds(at, 8), :],
            errors,
            (((0,), (0,)), ((), ())),
            precision=lax.Precision.HIGHEST,
            preferred_element_type=f32,
        )
        return carry

    lax.fori_loop(0, BLOCK // 8, group, 0)
    snapped_ref[...] = out[...].T
    errors_ref[...] = err[...].T


def block_update(rows, levels, pivots, panel_diag):
    whole = lambda *shape: pl.BlockSpec(shape, lambda i: (0,) * len(shape))
    count = rows.shape[0]
    return pl.pallas_call(
        columns_kernel,
        grid=(1,),
        in_specs=[
            whole(count, BLOCK),
            whole(1, count),
            pl.BlockSpec(memory_space=pltpu.SMEM),
            whole(BLOCK, BLOCK),
        ],
        out_specs=[whole(count, BLOCK)] * 2,
        out_shape=[jax.ShapeDtypeStruct((count, BLOCK), f32)] * 2,
        scratch_shapes=[pltpu.VMEM((BLOCK, count), f32)] * 3 + [pltpu.VMEM((BLOCK, BLOCK), f32)] * 2,
        compiler_params=pltpu.CompilerParams(vmem_limit_bytes=16 * MIB),
        cost_estimate=pl.CostEstimate(flops=10**9, bytes_accessed=2 * 10**6, transcendentals=0),
        name="block_update",
    )(pltpu.with_memory_space_constraint(rows, pltpu.HBM), levels, 1.0 / pivots, panel_diag)


def ahead_over_x(mine):
    return [mine] + [lax.ppermute(mine, "x", pairs) for pairs in (DOWN, OPPOSITE, UP)]


def later_kernel(here_ref, errors_ref, own_ref, other_ref, *refs):
    *weight_refs, out_ref, panel, parts = refs
    i = pl.program_id(0)
    wide = panel.shape[0] // 8
    count = errors_ref.shape[0]

    @pl.when(i == 0)
    def _():
        x, core = here_ref[0], here_ref[1]
        for at in range(4):
            ahead = lax.rem(at + 4 - x, 4)
            mine = pl.multiple_of((2 * at + core) * wide, 16)
            theirs = pl.multiple_of((2 * at + 1 - core) * wide, 16)
            panel[pl.ds(mine, wide), :] = own_ref[ahead, :wide, :]
            panel[pl.ds(theirs, wide), :] = other_ref[ahead, :wide, :]
        errors = errors_ref[...]
        for k in range(3):
            part = errors.astype(bf16)
            errors = errors - part.astype(f32)
            parts[k * count : (k + 1) * count, :] = part

    got = lax.dot_general(
        parts[...],
        panel[pl.ds(pl.multiple_of(i * 640, 128), 640), :],
        (((1,), (1,)), ((), ())),
        preferred_element_type=f32,
    )
    total = (got[:count] + got[count : 2 * count]) + got[2 * count :]
    for k, ref in enumerate(weight_refs):
        out_ref[:, k * 128 : (k + 1) * 128] = ref[...].astype(f32) - total[:, k * 128 : (k + 1) * 128]


def later_columns(here, rows, errors, own, other):
    count, later = rows.shape[0], rows.shape[1] - BLOCK
    columns = [
        pl.BlockSpec((count, 128), functools.partial(lambda k, i, here: (0, 5 * i + k), k))
        for k in range(1, 6)
    ]
    whole = lambda a: pl.BlockSpec(a.shape, lambda i, here: (0,) * a.ndim)
    return pl.pallas_call(
        later_kernel,
        grid_spec=pltpu.PrefetchScalarGridSpec(
            num_scalar_prefetch=1,
            grid=(later // 640,),
            in_specs=[whole(errors), whole(own), whole(other)] + columns,
            out_specs=pl.BlockSpec((count, 640), lambda i, here: (0, i)),
            scratch_shapes=[pltpu.VMEM((later, BLOCK), bf16), pltpu.VMEM((3 * count, BLOCK), bf16)],
        ),
        out_shape=pltpu.HBM((count, later), f32),
        compiler_params=pltpu.CompilerParams(vmem_limit_bytes=24 * MIB),
        cost_estimate=pl.CostEstimate(flops=15 * 10**8, bytes_accessed=13 * 10**6, transcendentals=0),
        name="later_columns",
    )(here, errors, own, other, *[pltpu.with_memory_space_constraint(rows, pltpu.HBM)] * 5)


def on_device(tokens, routes, weight, levels, pivots, panel_diag, panel_rest):
    x, core = lax.axis_index("x"), lax.axis_index("core")
    place = lax.axis_index("z") * 4 + lax.axis_index("y")
    exchange = functools.partial(
        lax.all_to_all, axis_name=PLANE, split_axis=0, concat_axis=0, tiled=True
    )
    here = jnp.stack([x, core]).astype(i32)

    first, second = build(tokens, routes.T)
    first, here, place, pivots = lax.optimization_barrier((first, here, place, pivots))
    first = exchange(first)
    first, second, weight, levels, panel_diag, panel_rest, pivots = lax.optimization_barrier(
        (first, second, weight, levels, panel_diag, panel_rest, pivots)
    )
    second = exchange(second)
    keep, send, top, slab, places = product0(here, first)
    keep, send, top, second, slab, places, panel_rest = lax.optimization_barrier(
        (keep, send, top, second, slab, places, panel_rest)
    )
    panel = ahead_over_x(panel_rest[0].T.astype(bf16))
    own, others = sum_over_core(keep, *over_core(send, top))
    places, second, slab, others = lax.optimization_barrier((places, second, slab, others))
    others = over_x(others)
    keep, send, top = product1(here, places, second, slab)
    keep, send, top, others, panel, weight = lax.optimization_barrier(
        (keep, send, top, others, panel, weight)
    )
    far_own, far_others = own, others
    own, others = sum_over_core(keep, *over_core(send, top))

    others, rows, panel, far_others = lax.optimization_barrier((others, weight[0], panel, far_others))
    others = over_x(others)
    total, least, counts = sum_over_x(far_own, far_others)
    snapped, errors = block_update(rows, levels, pivots[0], panel_diag[0])
    panel = jnp.stack(panel)
    other_panel = lax.ppermute(panel, "core", SWAP)
    others, errors, other_panel, total, least = lax.optimization_barrier(
        (others, errors, other_panel, total, least)
    )
    tail, last, _ = sum_over_x(own, others)
    sent = [total.reshape(EXPERTS, 128, 128), tail.reshape(EXPERTS, 96, 128)]
    first_rows = lax.broadcasted_iota(i32, (EXPERTS, 16, 128), 1) < 8
    sent.append(jnp.where(first_rows, least, last).astype(f16))
    sums = exchange(jnp.concatenate(sent, axis=1))

    remainder = later_columns(here, rows, errors, panel, other_panel)

    own_count = lax.dynamic_index_in_dim(counts[0], place, 0, keepdims=True)
    total = sums[:, :128].astype(f32) * jnp.exp2(-sums[:, 224:225].astype(f32))
    tail = sums[:, 128:224].astype(f32) * jnp.exp2(-sums[:, 232:233].astype(f32))
    hessian = put_in_order(2.0 / own_count, total, tail)
    return hessian[None], snapped[None], remainder[None]


def solution(mesh):
    devices = mesh.devices
    fine = Mesh(devices.reshape(4, 2, 4, 4), ("x", "core", "z", "y"))
    dp, every = ("x", "core"), ("x", "core", "z", "y")
    return jax.shard_map(
        on_device,
        mesh=fine,
        in_specs=(
            P(every, None),
            P(every, None),
            P(PLANE, dp, None),
            P(PLANE, dp),
            P(PLANE, None),
            P(PLANE, None, None),
            P(PLANE, None, dp),
        ),
        out_specs=(P(PLANE, dp, None),) * 3,
        check_vma=False,
    )
```
